32 devices in a mesh: gx: 2 (over y), gy: 4 (over x, core), gz: 4 (over z).
Axes of the slice: x: 2, y: 2, z: 4, core: 2. Of those that a mesh axis runs over, the one named last changes fastest.
Arguments:
- noise_vectors: bfloat16 [9, 4096, 128], P(None, ('gx', 'gy', 'gz')), may hold values from -6 to 6
- hamiltonian: bfloat16 [15, 9, 9, 4096], P(None, None, None, ('gx', 'gy', 'gz')), may hold values from -0.25 to 0.25
- derivative: bfloat16 [3, 15, 9, 9, 4096], P(None, None, None, None, ('gx', 'gy', 'gz')), may hold values from -0.625 to 0.625
- neighbours: int32 [4096, 15], P(('gx', 'gy', 'gz')), may hold values from 0 to 4095, as said below
- coefficients: float32 [4], replicated, may hold values from -1 to 1
Outputs:
- weighted: float32 [9, 4096, 128], P(None, ('gx', 'gy', 'gz'))
- forces: float32 [3, 4096], P(None, ('gx', 'gy', 'gz'))
The draws below stay inside these ranges and needn't reach their ends.
Inputs may be any that keep to these rules, and one draw needn't show every extreme that they name: `neighbours`: slot 0 of every atom's list is the atom itself; the other 14 slots name distinct other atoms whose cells differ from its own by at most one along each dimension, periodically on the grid of 8 x 16 x 16 cells with two atoms a cell. Atom ids run over domains in the order gx, gy, gz, each domain holding 128 atoms numbered by (atom of the cell, first, second, third cell index within the domain).
All inputs are finite; a program needn't handle non-finite values.
Results may differ from the reference program's by a relative error of at most 0.0003.
Values may be sent and summed in bfloat16 or wider, within the bound.
A program may use at most 128 MiB of HBM per device.

```python
import jax
import jax.numpy as jnp
from jax import lax

CX = 4
CY = 4
CZ = 4
NV = 128
ORB = 9
NEIGH = 15
ORDER = 3
NXC = 8
NYC = 16
NZC = 16
ATOM_DEV = 128
ATOMS = 4096
N_GY = 4
N_GZ = 4


def atom_place(atom_ids):
    cell_count = CX * CY * CZ
    domain = atom_ids // ATOM_DEV
    within = atom_ids % ATOM_DEV
    dom_x = domain // (N_GY * N_GZ)
    dom_y = domain // N_GZ % N_GY
    dom_z = domain % N_GZ
    basis_index = within // cell_count
    remain = within % cell_count
    cell_x = dom_x * CX + remain // (CY * CZ)
    cell_y = dom_y * CY + remain // CZ % CY
    cell_z = dom_z * CZ + remain % CZ
    return (basis_index, cell_x, cell_y, cell_z)


def atom_number(basis_index, cell_x, cell_y, cell_z):
    domain = (cell_x // CX * N_GY + cell_y // CY) * N_GZ + cell_z // CZ
    within = ((basis_index * CX + cell_x % CX) * CY + cell_y % CY) * CZ + cell_z % CZ
    return domain * ATOM_DEV + within


def draw_neighbours(key, part):
    key = jax.random.fold_in(key, 7)
    atom_ids = jnp.arange(ATOMS, dtype=jnp.int32)
    candidates = jnp.arange(54, dtype=jnp.int32)
    shift_x = candidates // 18 - 1
    shift_y = candidates // 6 % 3 - 1
    shift_z = candidates // 2 % 3 - 1
    cand_basis = candidates % 2
    basis_index, cell_x, cell_y, cell_z = atom_place(atom_ids)
    scores = jax.random.randint(key, (ATOMS, 54), 0, 1 << 20, dtype=jnp.int32) * 64 + candidates[None, :]
    is_self = (shift_x == 0) & (shift_y == 0) & (shift_z == 0)
    is_self = is_self[None, :] & (cand_basis[None, :] == basis_index[:, None])
    scores = jnp.where(is_self, jnp.int32(1 << 30), scores)
    ranking, chosen = lax.top_k(scores, NEIGH)
    part_x = jnp.remainder(cell_x[:, None] + shift_x[chosen], NXC)
    part_y = jnp.remainder(cell_y[:, None] + shift_y[chosen], NYC)
    part_z = jnp.remainder(cell_z[:, None] + shift_z[chosen], NZC)
    return atom_number(cand_basis[chosen], part_x, part_y, part_z).astype(jnp.int32)


def steps_of(stream_key, extent, cuts, low, top_value):
    def one(axis_at, shards_of):
        steps = jax.random.uniform(jax.random.fold_in(jax.random.fold_in(stream_key, 6), axis_at), (shards_of,), jnp.float32, low / len(cuts), top_value / len(cuts))
        return jnp.repeat(jnp.exp(steps), extent[axis_at] // shards_of).reshape((-1,) + (1,) * (len(extent) - axis_at - 1))

    gain = one(*cuts[0])
    for cut in cuts[1:]:
        gain = gain * one(*cut)
    return gain


def bell_draw(own_key, extent, spread, limit, split=(), held_as=jnp.bfloat16):
    entries = jax.random.normal(own_key, extent, jnp.float32) * spread
    if len(split) > 0:
        entries = steps_of(own_key, extent, split, -0.22, 0.18) * entries
    return jnp.clip(entries, min=-limit, max=limit).astype(held_as)


def setup_inputs(seed: int = 0) -> dict:
    key_of = jax.random.split(jax.random.key(seed), 6)
    noise_vectors = bell_draw(key_of[0], (ORB, ATOMS, NV), 1.0, 6.0, ((1, 32),))
    hamiltonian = bell_draw(key_of[1], (NEIGH, ORB, ORB, ATOMS), (4 * NEIGH * ORB) ** -0.5, 0.25, ((3, 32),))
    derivative = bell_draw(key_of[2], (3, NEIGH, ORB, ORB, ATOMS), (ORB * ORB) ** -0.5, 0.625, ((4, 32),))
    neighbours = draw_neighbours(jax.random.fold_in(key_of[5], 71), 0)
    coefficients = jnp.clip(jax.random.uniform(key_of[4], (ORDER + 1,), jnp.float32, -1.0, 1.0), -1.0, 1.0)
    return {"noise_vectors": noise_vectors, "hamiltonian": hamiltonian, "derivative": derivative, "neighbours": neighbours, "coefficients": coefficients}


def reference(noise_vectors, hamiltonian, derivative, neighbours, coefficients):
    highest = lax.Precision.HIGHEST

    def apply_blocks(vectors_in):
        summed = jnp.zeros(vectors_in.shape, jnp.float32)
        for slot_index in range(NEIGH):
            gathered = vectors_in[:, neighbours[:, slot_index]]
            blocks = hamiltonian[slot_index].astype(jnp.float32)
            summed = summed + jnp.einsum("abi,biv->aiv", blocks, gathered, precision=highest)
        return summed

    current = noise_vectors.astype(jnp.float32)
    result = coefficients[0] * current
    following = apply_blocks(current)
    result = result + coefficients[1] * following
    chain_prev = current
    chain_now = following
    for order_index in range(2, ORDER + 1):
        following = 2.0 * apply_blocks(chain_now) - chain_prev
        result = result + coefficients[order_index] * following
        chain_prev = chain_now
        chain_now = following

    forces = jnp.zeros((ATOMS, 3), jnp.float32)
    for slot_index in range(1, NEIGH):
        partner = neighbours[:, slot_index]
        gathered = current[:, partner]
        density = jnp.einsum("aiv,biv->iab", result, gathered, precision=highest) / NV
        pair_force = jnp.einsum("cabi,iab->ic", derivative[:, slot_index].astype(jnp.float32), density, precision=highest)
        forces = forces + jax.ops.segment_sum(pair_force, partner, num_segments=ATOMS) - pair_force
    return result, forces.T
```

```python
import functools

import jax
import jax.numpy as jnp
import numpy as np
from jax import lax
from jax.experimental import pallas as pl
from jax.experimental.pallas import tpu as pltpu
from jax.sharding import PartitionSpec as P

MESH = pl.DeviceIdType.MESH
CX = 4
CY = 4
CZ = 4
NEIGH = 15
ORB = 9
LANES = 128
GHOST = 384
EXT = LANES + GHOST
WIDE = ORB * LANES


def ghost_segments():
    found = []
    for dx in (-1, 0, 1):
        for dy in (-1, 0, 1):
            for dz in (-1, 0, 1):
                if (dx, dy, dz) != (0, 0, 0):
                    count = 2 * 4 ** ((dx == 0) + (dy == 0) + (dz == 0))
                    found.append(((dx, dy, dz), count))
    found.sort(key=lambda item: -item[1])
    placed = []
    row = 0
    for direction, count in found:
        rows = max(count, 8)
        placed.append((direction, row, rows))
        row += rows
    return placed, row


SEGMENTS, USED = ghost_segments()
COPIES = len(SEGMENTS)


def picking_matrix():
    picks = np.zeros((GHOST, LANES), np.float32)
    for (dx, dy, dz), first, _ in SEGMENTS:
        row = first
        for basis in range(2):
            for x in range(CX) if dx == 0 else ((0,) if dx > 0 else (CX - 1,)):
                for y in range(CY) if dy == 0 else ((0,) if dy > 0 else (CY - 1,)):
                    for z in range(CZ) if dz == 0 else ((0,) if dz > 0 else (CZ - 1,)):
                        picks[row, ((basis * CX + x) * CY + y) * CZ + z] = 1.0
                        row += 1
    return picks


def dot(a, b):
    return jnp.dot(a, b, preferred_element_type=jnp.float32)


def dot_t(a, b):
    return lax.dot_general(a, b, (((1,), (1,)), ((), ())), preferred_element_type=jnp.float32)


def halves(x):
    high = x.astype(jnp.bfloat16)
    return high, (x - high.astype(jnp.float32)).astype(jnp.bfloat16)


def kernel(
    sizes,
    noise,
    ham,
    deriv,
    index,
    coef,
    picks,
    w_out,
    f_out,
    ht_own,
    ht_ghost,
    onehot,
    ext_own,
    ext_ghost,
    noise_ext,
    gathered,
    chain,
    res,
    acc,
    sbuf,
    rbuf,
    fsend,
    frecv,
    pairs,
    dens,
    send_sem,
    recv_sem,
):
    f32 = jnp.float32
    bf16 = jnp.bfloat16
    here = [lax.axis_index(name) for name in ("gx", "gy", "gz")]

    def shifted(direction, sign):
        return tuple(
            lax.rem(me + size + sign * d, size) for me, size, d in zip(here, sizes, direction)
        )

    barrier = pltpu.get_barrier_semaphore()
    for direction, _, _ in SEGMENTS:
        pl.semaphore_signal(barrier, inc=1, device_id=shifted(direction, -1), device_id_type=MESH)
    for step in range(3):
        rbuf[step, :, USED:GHOST] = jnp.zeros((ORB, GHOST - USED, LANES), f32)
    frecv[USED:GHOST] = jnp.zeros((GHOST - USED, LANES), f32)
    for b in range(ORB):
        sbuf[0, b] = dot(picks[...], noise[b])
    pl.semaphore_wait(barrier, COPIES)

    def copies(step):
        made = []
        for at, (direction, first, rows) in enumerate(SEGMENTS):
            made.append(
                pltpu.make_async_remote_copy(
                    src_ref=sbuf.at[step, :, pl.ds(first, rows), :],
                    dst_ref=rbuf.at[step, :, pl.ds(first, rows), :],
                    send_sem=send_sem.at[step, at],
                    recv_sem=recv_sem.at[step, at],
                    device_id=shifted(direction, -1),
                    device_id_type=MESH,
                )
            )
        return made

    flying = [copies(step) for step in range(3)]
    for copy in flying[0]:
        copy.start()

    for b in range(ORB):
        turned = noise[b].astype(f32).T
        chain[0, :, b * LANES : (b + 1) * LANES] = turned
        ext_own[0:LANES, b * LANES : (b + 1) * LANES] = turned.astype(bf16)
        noise_ext[b * LANES : (b + 1) * LANES, 0:LANES] = turned.astype(bf16)

    @pl.loop(0, EXT // LANES)
    def _(part):
        first = pl.multiple_of(part * LANES, LANES)
        rows = lax.broadcasted_iota(jnp.int32, (LANES, LANES), 0) + first
        for m in range(NEIGH):
            same = rows == index[m : m + 1, :]
            onehot[pl.ds(first, LANES), m * LANES : (m + 1) * LANES] = jnp.where(
                same, 1.0, 0.0
            ).astype(bf16)

    def block_columns(a, first, store):
        rows = [ham[m, a].astype(f32) for m in range(NEIGH)]
        for b in range(ORB):
            total = None
            for m in range(NEIGH):
                row = jnp.broadcast_to(rows[m][b : b + 1], (16, LANES)).astype(bf16)
                hot = onehot[pl.ds(first, LANES), m * LANES : (m + 1) * LANES]
                term = hot.reshape(8, 16, LANES) * row[None]
                total = term if total is None else total + term
            store(b, total.reshape(LANES, LANES))

    @pl.loop(0, ORB)
    def _(a):
        columns = pl.ds(pl.multiple_of(a * LANES, LANES), LANES)

        def store_own(b, block):
            ht_own[b * LANES : (b + 1) * LANES, columns] = block

        block_columns(a, 0, store_own)

        @pl.loop(0, GHOST // LANES)
        def _(part):
            first = pl.multiple_of(part * LANES, LANES)

            def store_ghost(b, block):
                ht_ghost[pl.ds(b * GHOST + first, LANES), columns] = block

            block_columns(a, first + LANES, store_ghost)

    def multiply_own(rows):
        @pl.loop(0, 3)
        def _(part):
            columns = pl.ds(pl.multiple_of(part * GHOST, GHOST), GHOST)
            acc[0:rows, columns] = dot(ext_own[0:rows], ht_own[:, columns])

    def multiply_ghost(rows):
        @pl.loop(0, 3)
        def _(part):
            columns = pl.ds(pl.multiple_of(part * GHOST, GHOST), GHOST)
            acc[0:rows, columns] += dot(ext_ghost[0:rows], ht_ghost[:, columns])

    multiply_own(LANES)
    for copy in flying[0]:
        copy.wait_recv()
    for b in range(ORB):
        turned = rbuf[0, b].T.astype(bf16)
        ext_ghost[0:LANES, b * GHOST : (b + 1) * GHOST] = turned
        noise_ext[b * LANES : (b + 1) * LANES, LANES:EXT] = turned
    multiply_ghost(LANES)
    chain[1] = acc[0:LANES]
    res[...] = coef[0] * chain[0] + coef[1] * chain[1]

    def send_chain(step):
        high, low = halves(chain[step])
        ext_own[0:LANES] = high
        ext_own[LANES:] = low
        for b in range(ORB):
            cut = slice(b * LANES, (b + 1) * LANES)
            sbuf[step, b] = dot_t(picks[...], ext_own[0:LANES, cut]) + dot_t(
                picks[...], ext_own[LANES:, cut]
            )
        for copy in flying[step]:
            copy.start()

    def take_ghosts(step):
        for copy in flying[step]:
            copy.wait_recv()
        for b in range(ORB):
            high, low = halves(rbuf[step, b].T)
            ext_ghost[0:LANES, b * GHOST : (b + 1) * GHOST] = high
            ext_ghost[LANES:, b * GHOST : (b + 1) * GHOST] = low

    send_chain(1)
    multiply_own(2 * LANES)

    @pl.loop(0, (NEIGH - 1) // 2)
    def _(two):
        hot = onehot[:, pl.ds(pl.multiple_of(two * 2 * LANES + LANES, LANES), 2 * LANES)]
        both = dot(noise_ext[...], hot).astype(bf16)
        gathered[2 * two] = both[:, 0:LANES]
        gathered[2 * two + 1] = both[:, LANES:]

    take_ghosts(1)
    multiply_ghost(2 * LANES)
    chain[2] = 2.0 * (acc[0:LANES] + acc[LANES:]) - chain[0]
    res[...] += coef[2] * chain[2]

    send_chain(2)
    multiply_own(2 * LANES)
    take_ghosts(2)
    multiply_ghost(2 * LANES)
    res[...] += coef[3] * (2.0 * (acc[0:LANES] + acc[LANES:]) - chain[1])

    for a in range(ORB):
        w_out[a] = res[:, a * LANES : (a + 1) * LANES].T

    pairs[...] = jnp.zeros(pairs.shape, f32)

    @pl.loop(1, NEIGH)
    def _(m):
        columns = pl.ds(pl.multiple_of(m * LANES, LANES), LANES)
        for b in range(ORB):
            near = gathered[m - 1, b * LANES : (b + 1) * LANES].astype(f32)
            for a in range(ORB):
                term = res[:, a * LANES : (a + 1) * LANES] * near
                dens[a, b : b + 1] = jnp.sum(term, axis=0, keepdims=True)
        for c in range(3):
            total = deriv[c, m, 0].astype(f32) * dens[0]
            for a in range(1, ORB):
                total = total + deriv[c, m, a].astype(f32) * dens[a]
            pair = jnp.sum(total, axis=0, keepdims=True) * (1.0 / LANES)
            pairs[c : c + 1, columns] = pair
            pairs[c : c + 1, 0:LANES] -= pair

    high, low = halves(pairs[...])
    stacked = jnp.concatenate(
        [high, low, jnp.zeros((LANES - 16, NEIGH * LANES), bf16)], axis=0
    )
    spread = dot_t(onehot[...], stacked)
    fsend[...] = spread[LANES:EXT]

    back = []
    for at, (direction, first, rows) in enumerate(SEGMENTS):
        back.append(
            pltpu.make_async_remote_copy(
                src_ref=fsend.at[pl.ds(first, rows), :],
                dst_ref=frecv.at[pl.ds(first, rows), :],
                send_sem=send_sem.at[3, at],
                recv_sem=recv_sem.at[3, at],
                device_id=shifted(direction, 1),
                device_id_type=MESH,
            )
        )
    for copy in back:
        copy.start()
    own = spread[0:LANES].T[0:16]
    for copy in back:
        copy.wait_recv()
    high, low = halves(frecv[...].T[0:16])
    total = own + dot(high, picks[...]) + dot(low, picks[...])
    f_out[...] = total[0:3] + total[8:11]
    for copy in flying[0] + flying[1] + flying[2] + back:
        copy.wait_send()


def extended_slots(sizes, neighbours):
    atom_count = neighbours.shape[0]
    cell_count = CX * CY * CZ
    size_x, size_y, size_z = sizes
    ids = neighbours.T
    domain = ids // atom_count
    within = ids % atom_count
    basis = within // cell_count
    remain = within % cell_count
    parts = (
        (domain // (size_y * size_z), remain // (CY * CZ), "gx", CX, size_x),
        (domain // size_z % size_y, remain // CZ % CY, "gy", CY, size_y),
        (domain % size_z, remain % CZ, "gz", CZ, size_z),
    )
    signs = []
    inside = basis
    for dom, cell, axis, cells, size in parts:
        place = jnp.remainder((dom - lax.axis_index(axis)) * cells + cell + 1, cells * size)
        sign = jnp.where(place == 0, -1, jnp.where(place == cells + 1, 1, 0))
        signs.append(sign)
        inside = jnp.where(sign == 0, inside * cells + place - 1, inside)
    code = signs[0] * 9 + signs[1] * 3 + signs[2]
    first = jnp.zeros_like(code)
    for (dx, dy, dz), row, _ in SEGMENTS:
        first = jnp.where(code == dx * 9 + dy * 3 + dz, LANES + row, first)
    slots = first + inside
    return jnp.concatenate([slots, jnp.full((1, atom_count), -1, jnp.int32)], axis=0)


def shards(sizes, noise, ham, deriv, neighbours, coef):
    f32 = jnp.float32
    bf16 = jnp.bfloat16
    index = extended_slots(sizes, neighbours)
    picks = jnp.asarray(picking_matrix(), bf16)
    vmem = pl.BlockSpec(memory_space=pltpu.VMEM)
    smem = pl.BlockSpec(memory_space=pltpu.SMEM)
    return pl.pallas_call(
        functools.partial(kernel, sizes),
        out_shape=(
            jax.ShapeDtypeStruct((ORB, LANES, LANES), f32),
            jax.ShapeDtypeStruct((3, LANES), f32),
        ),
        in_specs=[vmem, vmem, vmem, vmem, smem, vmem],
        out_specs=(vmem, vmem),
        scratch_shapes=[
            pltpu.VMEM((ORB * LANES, WIDE), bf16),
            pltpu.VMEM((ORB * GHOST, WIDE), bf16),
            pltpu.VMEM((EXT, NEIGH * LANES), bf16),
            pltpu.VMEM((2 * LANES, ORB * LANES), bf16),
            pltpu.VMEM((2 * LANES, ORB * GHOST), bf16),
            pltpu.VMEM((WIDE, EXT), bf16),
            pltpu.VMEM((NEIGH - 1, WIDE, LANES), bf16),
            pltpu.VMEM((3, LANES, WIDE), f32),
            pltpu.VMEM((LANES, WIDE), f32),
            pltpu.VMEM((2 * LANES, WIDE), f32),
            pltpu.VMEM((3, ORB, GHOST, LANES), f32),
            pltpu.VMEM((3, ORB, GHOST, LANES), f32),
            pltpu.VMEM((GHOST, LANES), f32),
            pltpu.VMEM((GHOST, LANES), f32),
            pltpu.VMEM((8, NEIGH * LANES), f32),
            pltpu.VMEM((ORB, ORB, LANES), f32),
            pltpu.SemaphoreType.DMA((4, COPIES)),
            pltpu.SemaphoreType.DMA((4, COPIES)),
        ],
        compiler_params=pltpu.CompilerParams(
            collective_id=0, has_side_effects=True, vmem_limit_bytes=56 * 1024 * 1024
        ),
        name="fermi_forces",
    )(noise, ham, deriv, index, coef, picks)


def solution(mesh):
    sizes = tuple(mesh.shape[name] for name in ("gx", "gy", "gz"))
    in_specs = (
        P(None, ("gx", "gy", "gz"), None),
        P(None, None, None, ("gx", "gy", "gz")),
        P(None, None, None, None, ("gx", "gy", "gz")),
        P(("gx", "gy", "gz"), None),
        P(),
    )
    out_specs = (P(None, ("gx", "gy", "gz"), None), P(None, ("gx", "gy", "gz")))
    return jax.shard_map(
        functools.partial(shards, sizes),
        mesh=mesh,
        in_specs=in_specs,
        out_specs=out_specs,
        check_vma=False,
    )
```

```python
import functools

import jax
import jax.numpy as jnp
import numpy as np
from jax import lax
from jax.experimental import pallas as pl
from jax.experimental.pallas import tpu as pltpu
from jax.sharding import PartitionSpec as P

MESH = pl.DeviceIdType.MESH
CX = 4
CY = 4
CZ = 4
NEIGH = 15
ORB = 9
LANES = 128
HALF = 64
WIDE = ORB * LANES
FACE = 32
EDGE = 8
CORNER = 2
FACES = 6
EDGES = 12
CORNERS = 8
PICKED = FACES * FACE + EDGES * EDGE + CORNERS * CORNER
EXT = 512
FACE_ROWS = ORB * FACE
EDGE_ROWS = 80
CORNER_ROWS = 32
EDGE_AT = FACES * FACE_ROWS
CORNER_AT = EDGES * EDGE_ROWS
SMALL = CORNER_AT + CORNERS * CORNER_ROWS
GHOST = EDGE_AT + SMALL
SHARE = 384


def ghost_segments():
    kinds = ([], [], [])
    for dx in (-1, 0, 1):
        for dy in (-1, 0, 1):
            for dz in (-1, 0, 1):
                axes = abs(dx) + abs(dy) + abs(dz)
                if axes > 0:
                    kinds[axes - 1].append((dx, dy, dz))
    placed = []
    picked = 0
    sent = 0
    for group, atoms, rows in zip(
        kinds, (FACE, EDGE, CORNER), (FACE_ROWS, EDGE_ROWS, CORNER_ROWS)
    ):
        for direction in group:
            placed.append((direction, picked, sent, rows))
            picked += atoms
            sent += rows
    return placed


SEGMENTS = ghost_segments()
COPIES = len(SEGMENTS)


def picking_matrix():
    picks = np.zeros((PICKED, LANES), np.float32)
    for (dx, dy, dz), first, _, _ in SEGMENTS:
        row = first
        for basis in range(2):
            for x in range(CX) if dx == 0 else ((0,) if dx > 0 else (CX - 1,)):
                for y in range(CY) if dy == 0 else ((0,) if dy > 0 else (CY - 1,)):
                    for z in range(CZ) if dz == 0 else ((0,) if dz > 0 else (CZ - 1,)):
                        picks[row, ((basis * CX + x) * CY + y) * CZ + z] = 1.0
                        row += 1
    return picks


def segment_spans():
    spans = np.zeros((COPIES, 8, SHARE), np.float32)
    for at, (direction, first, _, _) in enumerate(SEGMENTS):
        axes = sum(abs(d) for d in direction)
        spans[at, :, first : first + (FACE, EDGE, CORNER)[axes - 1]] = 1.0
    return spans


def dot(a, b):
    return jnp.dot(a, b, preferred_element_type=jnp.float32)


def dot_t(a, b):
    return lax.dot_general(a, b, (((1,), (1,)), ((), ())), preferred_element_type=jnp.float32)


def halves(x):
    high = x.astype(jnp.bfloat16)
    return high, (x - high.astype(jnp.float32)).astype(jnp.bfloat16)


def kernel(
    sizes,
    noise,
    ham,
    deriv,
    index,
    coef,
    picks,
    spans,
    w_out,
    f_out,
    ht_own,
    ht_ghost,
    onehot,
    ext_own,
    ext_ghost,
    noise_ext,
    gathered,
    chain,
    res,
    acc,
    sbuf,
    rbuf,
    small,
    small_ham,
    fsend,
    frecv,
    pairs,
    dens,
    send_sem,
    recv_sem,
):
    f32 = jnp.float32
    bf16 = jnp.bfloat16
    here = [lax.axis_index(name) for name in ("gx", "gy", "gz")]

    def shifted(direction, sign):
        return tuple(
            lax.rem(me + size + sign * d, size) for me, size, d in zip(here, sizes, direction)
        )

    barrier = pltpu.get_barrier_semaphore()
    for direction, _, _, _ in SEGMENTS:
        pl.semaphore_signal(barrier, inc=1, device_id=shifted(direction, -1), device_id_type=MESH)

    def pack(step, rows_of):
        for b in range(ORB):
            rows = rows_of(b)
            for f in range(FACES):
                to = (f * ORB + b) * FACE
                sbuf[step, to : to + FACE] = rows[f * FACE : (f + 1) * FACE].astype(bf16)
            for e in range(EDGES):
                at = FACES * FACE + e * EDGE
                to = e * EDGE_ROWS + b * EDGE
                small[to : to + EDGE] = rows[at : at + EDGE]
            for c in range(CORNERS):
                at = FACES * FACE + EDGES * EDGE + c * CORNER
                to = CORNER_AT + c * CORNER_ROWS + b * CORNER
                small[to : to + CORNER] = rows[at : at + CORNER]
        sbuf[step, EDGE_AT:GHOST] = small[...].astype(bf16)

    def copies(step):
        made = []
        for at, (direction, _, first, rows) in enumerate(SEGMENTS):
            made.append(
                pltpu.make_async_remote_copy(
                    src_ref=sbuf.at[step, pl.ds(first, rows), :],
                    dst_ref=rbuf.at[step, pl.ds(first, rows), :],
                    send_sem=send_sem.at[step, at],
                    recv_sem=recv_sem.at[step, at],
                    device_id=shifted(direction, -1),
                    device_id_type=MESH,
                )
            )
        return made

    flying = [copies(step) for step in range(5)]

    small[...] = jnp.zeros(small.shape, f32)
    small_ham[...] = jnp.zeros(small_ham.shape, f32)
    pack(0, lambda b: dot(picks[...], noise[b]))
    pl.semaphore_wait(barrier, COPIES)
    for copy in flying[0]:
        copy.start()

    for b in range(ORB):
        turned = noise[b].astype(f32).T
        chain[0, :, b * LANES : (b + 1) * LANES] = turned
        ext_own[0:LANES, b * LANES : (b + 1) * LANES] = turned.astype(bf16)
        noise_ext[b * LANES : (b + 1) * LANES, 0:LANES] = turned.astype(bf16)

    @pl.loop(0, EXT // LANES)
    def _(part):
        first = pl.multiple_of(part * LANES, LANES)
        rows = lax.broadcasted_iota(jnp.int32, (LANES, LANES), 0) + first
        for m in range(NEIGH):
            same = rows == index[m : m + 1, :]
            onehot[pl.ds(first, LANES), m * LANES : (m + 1) * LANES] = jnp.where(
                same, 1.0, 0.0
            ).astype(bf16)

    @pl.loop(0, ORB)
    def _(a):
        columns = pl.ds(pl.multiple_of(a * LANES, LANES), LANES)
        for b in range(ORB):
            blocks = ham[a, b].astype(f32)
            rows = [
                jnp.broadcast_to(blocks[m : m + 1], (16, LANES)).astype(bf16)[None]
                for m in range(NEIGH)
            ]

            def block(first, count):
                total = None
                for m in range(NEIGH):
                    hot = onehot[first : first + count, m * LANES : (m + 1) * LANES]
                    term = hot.reshape(count // 16, 16, LANES) * rows[m]
                    total = term if total is None else total + term
                return total.reshape(count, LANES)

            ht_own[b * LANES : (b + 1) * LANES, columns] = block(0, LANES)
            for two in range(FACES // 2):
                made = block(LANES + two * 2 * FACE, 2 * FACE)
                for f in (2 * two, 2 * two + 1):
                    to = (f * ORB + b) * FACE
                    ht_ghost[to : to + FACE, columns] = made[(f % 2) * FACE : (f % 2 + 1) * FACE]
            made = block(LANES + FACES * FACE, EDGES * EDGE + CORNERS * CORNER).astype(f32)
            for e in range(EDGES):
                to = e * EDGE_ROWS + b * EDGE
                small_ham[to : to + EDGE] = made[e * EDGE : (e + 1) * EDGE]
            for c in range(CORNERS):
                at = EDGES * EDGE + c * CORNER
                to = CORNER_AT + c * CORNER_ROWS + b * CORNER
                small_ham[to : to + CORNER] = made[at : at + CORNER]
        ht_ghost[EDGE_AT:GHOST, columns] = small_ham[...].astype(bf16)

    def multiply(rows, ext, operator, first):
        @pl.loop(0, 3)
        def _(part):
            columns = pl.ds(pl.multiple_of(part * SHARE, SHARE), SHARE)
            product = dot(ext[rows], operator[:, columns])
            if first:
                acc[rows, columns] = product
            else:
                acc[rows, columns] += product

    def take(step, rows):
        for copy in flying[step]:
            copy.wait_recv()
        ext_ghost[rows] = rbuf[step].T

    vectors = (slice(0, HALF), slice(HALF, LANES))
    pieces = (slice(0, LANES), slice(LANES, 2 * LANES))

    def summed(half):
        base = half * LANES
        return acc[base : base + HALF] + acc[base + HALF : base + LANES]

    def send_half(order, half):
        high, low = halves(chain[order, vectors[half]])
        ext_own[half * LANES : half * LANES + HALF] = high
        ext_own[half * LANES + HALF : (half + 1) * LANES] = low
        step = 2 * order - 1 + half
        pack(
            step,
            lambda b: dot_t(picks[...], ext_own[pieces[half], b * LANES : (b + 1) * LANES]),
        )
        for copy in flying[step]:
            copy.start()

    multiply(pieces[0], ext_own, ht_own, True)
    take(0, pieces[0])
    multiply(pieces[0], ext_ghost, ht_ghost, False)
    chain[1] = acc[0:LANES]
    send_half(1, 0)
    send_half(1, 1)
    res[...] = coef[0] * chain[0] + coef[1] * chain[1]

    for b in range(ORB):
        parts = []
        for f in range(FACES):
            at = (f * ORB + b) * FACE
            parts.append(rbuf[0, at : at + FACE])
        noise_rows = jnp.concatenate(parts, axis=0)
        noise_ext[b * LANES : (b + 1) * LANES, LANES : LANES + FACES * FACE] = noise_rows.T
    small[...] = rbuf[0, EDGE_AT:GHOST].astype(f32)
    for b in range(ORB):
        parts = []
        for e in range(EDGES):
            at = e * EDGE_ROWS + b * EDGE
            parts.append(small[at : at + EDGE])
        for c in range(CORNERS):
            at = CORNER_AT + c * CORNER_ROWS + b * CORNER
            parts.append(small[at : at + CORNER])
        parts.append(jnp.zeros((EXT - LANES - PICKED, LANES), f32))
        noise_rows = jnp.concatenate(parts, axis=0).astype(bf16)
        noise_ext[b * LANES : (b + 1) * LANES, LANES + FACES * FACE : EXT] = noise_rows.T

    multiply(slice(0, 2 * LANES), ext_own, ht_own, True)

    @pl.loop(0, (NEIGH - 1) // 2)
    def _(two):
        hot = onehot[:, pl.ds(pl.multiple_of(two * 2 * LANES + LANES, LANES), 2 * LANES)]
        both = dot(noise_ext[...], hot).astype(bf16)
        gathered[2 * two] = both[:, 0:LANES]
        gathered[2 * two + 1] = both[:, LANES:]

    for half in range(2):
        take(1 + half, pieces[half])
        multiply(pieces[half], ext_ghost, ht_ghost, False)
        chain[2, vectors[half]] = 2.0 * summed(half) - chain[0, vectors[half]]
        send_half(2, half)
        multiply(pieces[half], ext_own, ht_own, True)
    res[...] += coef[2] * chain[2]

    dens[:, 0:1] = jnp.zeros((ORB * ORB, 1, LANES), f32)

    for half in range(2):
        take(3 + half, pieces[half])
        multiply(pieces[half], ext_ghost, ht_ghost, False)
        res[vectors[half]] += coef[3] * (2.0 * summed(half) - chain[1, vectors[half]])

        @pl.loop(1, NEIGH)
        def _(m):
            for b in range(ORB):
                base = b * LANES + half * HALF
                near = gathered[m - 1, base : base + HALF].astype(f32)
                for a in range(ORB):
                    term = res[vectors[half], a * LANES : (a + 1) * LANES] * near
                    row = jnp.sum(term, axis=0, keepdims=True)
                    if half == 0:
                        dens[a * ORB + b, pl.ds(m, 1)] = row
                    else:
                        dens[a * ORB + b, pl.ds(m, 1)] += row

    pairs[...] = jnp.zeros(pairs.shape, f32)
    for c in range(3):
        def add(ab, total):
            return total + deriv[c, ab].astype(f32) * dens[ab, 0:NEIGH]

        total = lax.fori_loop(0, ORB * ORB, add, jnp.zeros((NEIGH, LANES), f32), unroll=9)
        pair = total * (1.0 / LANES)
        pairs[c : c + 1, 0:LANES] = -jnp.sum(pair, axis=0, keepdims=True)
        for m in range(1, NEIGH):
            pairs[c : c + 1, m * LANES : (m + 1) * LANES] = pair[m : m + 1]
    high, low = halves(pairs[...])
    spread = dot_t(jnp.concatenate([high, low], axis=0), onehot[...])
    spread = spread[0:8] + spread[8:16]
    high, low = halves(spread[:, LANES:EXT])
    mask = spans[...]
    shape = (COPIES * 8, SHARE)
    high = (high.astype(f32)[None] * mask).reshape(shape).astype(bf16)
    low = (low.astype(f32)[None] * mask).reshape(shape).astype(bf16)
    tiles = dot(high[:, 0:PICKED], picks[...]) + dot(low[:, 0:PICKED], picks[...])
    fsend[...] = tiles.reshape(COPIES, 8, LANES)

    back = []
    for at, (direction, _, _, _) in enumerate(SEGMENTS):
        back.append(
            pltpu.make_async_remote_copy(
                src_ref=fsend.at[at],
                dst_ref=frecv.at[at],
                send_sem=send_sem.at[5, at],
                recv_sem=recv_sem.at[5, at],
                device_id=shifted(direction, 1),
                device_id_type=MESH,
            )
        )
    for copy in back:
        copy.start()
    for a in range(ORB):
        w_out[a] = res[:, a * LANES : (a + 1) * LANES].T
    for copy in back:
        copy.wait_recv()
    total = spread[:, 0:LANES]
    for at in range(COPIES):
        total = total + frecv[at]
    f_out[...] = total[0:3]
    for group in flying:
        for copy in group:
            copy.wait_send()
    for copy in back:
        copy.wait_send()


def extended_slots(sizes, neighbours):
    atom_count = neighbours.shape[0]
    cell_count = CX * CY * CZ
    size_x, size_y, size_z = sizes
    ids = neighbours.T
    domain = ids // atom_count
    within = ids % atom_count
    basis = within // cell_count
    remain = within % cell_count
    parts = (
        (domain // (size_y * size_z), remain // (CY * CZ), "gx", CX, size_x),
        (domain // size_z % size_y, remain // CZ % CY, "gy", CY, size_y),
        (domain % size_z, remain % CZ, "gz", CZ, size_z),
    )
    signs = []
    inside = basis
    for dom, cell, axis, cells, size in parts:
        place = jnp.remainder((dom - lax.axis_index(axis)) * cells + cell + 1, cells * size)
        sign = jnp.where(place == 0, -1, jnp.where(place == cells + 1, 1, 0))
        signs.append(sign)
        inside = jnp.where(sign == 0, inside * cells + place - 1, inside)
    code = signs[0] * 9 + signs[1] * 3 + signs[2]
    first = jnp.zeros_like(code)
    for (dx, dy, dz), row, _, _ in SEGMENTS:
        first = jnp.where(code == dx * 9 + dy * 3 + dz, LANES + row, first)
    return first + inside


def shards(sizes, noise, ham, deriv, neighbours, coef):
    f32 = jnp.float32
    bf16 = jnp.bfloat16
    index = extended_slots(sizes, neighbours)
    ham = ham.transpose(1, 2, 0, 3)
    deriv = deriv.transpose(0, 2, 3, 1, 4).reshape(3, ORB * ORB, NEIGH, LANES)
    picks = jnp.asarray(picking_matrix(), bf16)
    spans = jnp.asarray(segment_spans(), f32)
    vmem = pl.BlockSpec(memory_space=pltpu.VMEM)
    smem = pl.BlockSpec(memory_space=pltpu.SMEM)
    return pl.pallas_call(
        functools.partial(kernel, sizes),
        out_shape=(
            jax.ShapeDtypeStruct((ORB, LANES, LANES), f32),
            jax.ShapeDtypeStruct((3, LANES), f32),
        ),
        in_specs=[vmem, vmem, vmem, vmem, smem, vmem, vmem],
        out_specs=(vmem, vmem),
        scratch_shapes=[
            pltpu.VMEM((WIDE, WIDE), bf16),
            pltpu.VMEM((GHOST, WIDE), bf16),
            pltpu.VMEM((EXT, NEIGH * LANES), bf16),
            pltpu.VMEM((2 * LANES, WIDE), bf16),
            pltpu.VMEM((2 * LANES, GHOST), bf16),
            pltpu.VMEM((WIDE, EXT), bf16),
            pltpu.VMEM((NEIGH - 1, WIDE, LANES), bf16),
            pltpu.VMEM((3, LANES, WIDE), f32),
            pltpu.VMEM((LANES, WIDE), f32),
            pltpu.VMEM((2 * LANES, WIDE), f32),
            pltpu.VMEM((5, GHOST, LANES), bf16),
            pltpu.VMEM((5, GHOST, LANES), bf16),
            pltpu.VMEM((SMALL, LANES), f32),
            pltpu.VMEM((SMALL, LANES), f32),
            pltpu.VMEM((COPIES, 8, LANES), f32),
            pltpu.VMEM((COPIES, 8, LANES), f32),
            pltpu.VMEM((8, NEIGH * LANES), f32),
            pltpu.VMEM((ORB * ORB, 16, LANES), f32),
            pltpu.SemaphoreType.DMA((6, COPIES)),
            pltpu.SemaphoreType.DMA((6, COPIES)),
        ],
        compiler_params=pltpu.CompilerParams(
            collective_id=0, has_side_effects=True, vmem_limit_bytes=56 * 1024 * 1024
        ),
        name="fermi_forces",
    )(noise, ham, deriv, index, coef, picks, spans)


def solution(mesh):
    sizes = tuple(mesh.shape[name] for name in ("gx", "gy", "gz"))
    in_specs = (
        P(None, ("gx", "gy", "gz"), None),
        P(None, None, None, ("gx", "gy", "gz")),
        P(None, None, None, None, ("gx", "gy", "gz")),
        P(("gx", "gy", "gz"), None),
        P(),
    )
    out_specs = (P(None, ("gx", "gy", "gz"), None), P(None, ("gx", "gy", "gz")))
    return jax.shard_map(
        functools.partial(shards, sizes),
        mesh=mesh,
        in_specs=in_specs,
        out_specs=out_specs,
        check_vma=False,
    )
```

```python
import functools

import jax
import jax.numpy as jnp
import numpy as np
from jax import lax
from jax.experimental import pallas as pl
from jax.experimental.pallas import tpu as pltpu
from jax.sharding import PartitionSpec as P

MESH = pl.DeviceIdType.MESH
CX = 4
CY = 4
CZ = 4
NEIGH = 15
ORB = 9
LANES = 128
HALF = 64
WIDE = ORB * LANES
FACE = 32
EDGE = 8
CORNER = 2
FACES = 6
EDGES = 4
DIRECT = FACES * FACE + EDGES * EDGE
RELAY = 4 * EDGE + 4 * CORNER
PICKED = DIRECT + 2 * RELAY
EXT = 512
FACE_ROWS = ORB * FACE
EDGE_ROWS = 80
RELAY_ROWS = 368
EDGE_AT = FACES * FACE_ROWS
RELAY_AT = EDGE_AT + EDGES * EDGE_ROWS
SENT = RELAY_AT + 2 * RELAY_ROWS
GHOST = SENT + 32
SMALL = GHOST - EDGE_AT
SHARE = 384
HELD = ((-1, 0, 0), (1, 0, 0), (0, 0, -1), (0, 0, 1), (-1, 0, -1), (-1, 0, 1), (1, 0, -1), (1, 0, 1))


def ghost_segments():
    order = HELD[0:4] + ((0, -1, 0), (0, 1, 0)) + HELD[4:8]
    for dy in (-1, 1):
        order = order + tuple((dx, dy, dz) for dx, _, dz in HELD)
    placed = []
    first = 0
    for direction in order:
        placed.append((direction, first, atoms_in(direction)))
        first += atoms_in(direction)
    return placed


def atoms_in(direction):
    return (FACE, EDGE, CORNER)[sum(abs(d) for d in direction) - 1]


SEGMENTS = ghost_segments()
COPIES = len(SEGMENTS)


def cells_of(d, cells):
    return range(cells) if d == 0 else ((0,) if d > 0 else (cells - 1,))


def picking_matrix():
    picks = np.zeros((PICKED, LANES), np.float32)
    row = 0
    for (dx, dy, dz), _, _ in SEGMENTS:
        for basis in range(2):
            for x in cells_of(dx, CX):
                for y in cells_of(dy, CY):
                    for z in cells_of(dz, CZ):
                        picks[row, ((basis * CX + x) * CY + y) * CZ + z] = 1.0
                        row += 1
    return picks


def relaying_matrix():
    picks = np.zeros((2 * RELAY, 4 * FACE + 4 * EDGE), np.float32)
    row = 0
    for dy in (-1, 1):
        held = 0
        for dx, _, dz in HELD:
            for basis in range(2):
                for x in cells_of(dx, CX):
                    for y in range(CY):
                        for z in cells_of(dz, CZ):
                            if y in cells_of(dy, CY):
                                picks[row, held] = 1.0
                                row += 1
                            held += 1
    return picks


def segment_spans():
    spans = np.zeros((COPIES, 8, SHARE), np.float32)
    for at, (_, first, count) in enumerate(SEGMENTS):
        spans[at, :, first : first + count] = 1.0
    return spans


def dot(a, b):
    return jnp.dot(a, b, preferred_element_type=jnp.float32)


def dot_t(a, b):
    return lax.dot_general(a, b, (((1,), (1,)), ((), ())), preferred_element_type=jnp.float32)


def halves(x):
    high = x.astype(jnp.bfloat16)
    return high, (x - high.astype(jnp.float32)).astype(jnp.bfloat16)


def kernel(
    sizes,
    noise,
    ham,
    deriv,
    index,
    coef,
    picks,
    relays,
    spans,
    w_out,
    f_out,
    ht_own,
    ht_ghost,
    onehot,
    ext_own,
    ext_ghost,
    noise_ext,
    gathered,
    chain,
    res,
    acc,
    sbuf,
    rbuf,
    small,
    small_ham,
    small_relay,
    near_slot,
    far_slot,
    fsend,
    frecv,
    pairs,
    dens,
    send_sem,
    recv_sem,
):
    f32 = jnp.float32
    bf16 = jnp.bfloat16
    here = [lax.axis_index(name) for name in ("gx", "gy", "gz")]

    def shifted(direction, sign):
        return tuple(
            lax.rem(me + size + sign * d, size) for me, size, d in zip(here, sizes, direction)
        )

    barrier = pltpu.get_barrier_semaphore()
    for direction, _, _ in SEGMENTS:
        pl.semaphore_signal(barrier, inc=1, device_id=shifted(direction, -1), device_id_type=MESH)

    def pack(step, rows_of):
        for b in range(ORB):
            rows = rows_of(b)
            for f in range(FACES):
                to = (f * ORB + b) * FACE
                sbuf[step, to : to + FACE] = rows[f * FACE : (f + 1) * FACE].astype(bf16)
            for e in range(EDGES):
                at = FACES * FACE + e * EDGE
                to = e * EDGE_ROWS + b * EDGE
                small[to : to + EDGE] = rows[at : at + EDGE]
        sbuf[step, EDGE_AT:RELAY_AT] = small[0 : EDGES * EDGE_ROWS].astype(bf16)

    def copy_rows(step, at, first, rows, direction):
        return pltpu.make_async_remote_copy(
            src_ref=sbuf.at[step, pl.ds(first, rows), :],
            dst_ref=rbuf.at[step, pl.ds(first, rows), :],
            send_sem=send_sem.at[step, at],
            recv_sem=recv_sem.at[step, at],
            device_id=shifted(direction, -1),
            device_id_type=MESH,
        )

    def copies(step):
        made = []
        for at, (direction, _, _) in enumerate(SEGMENTS[0 : FACES + EDGES]):
            if at < FACES:
                made.append(copy_rows(step, at, at * FACE_ROWS, FACE_ROWS, direction))
            else:
                first = EDGE_AT + (at - FACES) * EDGE_ROWS
                made.append(copy_rows(step, at, first, EDGE_ROWS, direction))
        return made

    def relay_copies(step):
        made = []
        for at, dy in enumerate((-1, 1)):
            first = RELAY_AT + at * RELAY_ROWS
            made.append(copy_rows(step, FACES + EDGES + at, first, RELAY_ROWS, (0, dy, 0)))
        return made

    flying = [copies(step) for step in range(5)]
    relayed = [relay_copies(step) for step in range(5)]

    def pass_on(step):
        for copy in flying[step]:
            copy.wait_recv()
        edges = rbuf[step, EDGE_AT:RELAY_AT].astype(f32)
        for b in range(ORB):
            parts = []
            for f in range(4):
                at = (f * ORB + b) * FACE
                parts.append(rbuf[step, at : at + FACE])
            lines = []
            for e in range(EDGES):
                at = e * EDGE_ROWS + b * EDGE
                lines.append(edges[at : at + EDGE])
            parts.append(jnp.concatenate(lines, axis=0).astype(bf16))
            rows = dot(relays[...], jnp.concatenate(parts, axis=0))
            for side in range(2):
                to = side * RELAY_ROWS + b * RELAY
                small_relay[to : to + RELAY] = rows[side * RELAY : (side + 1) * RELAY]
        sbuf[step, RELAY_AT:SENT] = small_relay[...].astype(bf16)
        for copy in relayed[step]:
            copy.start()

    small[...] = jnp.zeros(small.shape, f32)
    small_ham[...] = jnp.zeros(small_ham.shape, f32)
    small_relay[...] = jnp.zeros(small_relay.shape, f32)
    for step in range(5):
        rbuf[step, SENT:GHOST] = jnp.zeros((GHOST - SENT, LANES), bf16)
    pack(0, lambda b: dot(picks[0:DIRECT], noise[b]))
    pl.semaphore_wait(barrier, COPIES)
    for copy in flying[0]:
        copy.start()

    for b in range(ORB):
        turned = noise[b].astype(f32).T
        chain[0, :, b * LANES : (b + 1) * LANES] = turned
        ext_own[0:LANES, b * LANES : (b + 1) * LANES] = turned.astype(bf16)
        noise_ext[b * LANES : (b + 1) * LANES, 0:LANES] = turned.astype(bf16)

    @pl.loop(0, EXT // LANES)
    def _(part):
        first = pl.multiple_of(part * LANES, LANES)
        rows = lax.broadcasted_iota(jnp.int32, (LANES, LANES), 0) + first
        for m in range(NEIGH):
            same = rows == index[m : m + 1, :]
            onehot[pl.ds(first, LANES), m * LANES : (m + 1) * LANES] = jnp.where(
                same, 1.0, 0.0
            ).astype(bf16)

    @pl.loop(0, (LANES + PICKED) // 8)
    def _(part):
        first = pl.multiple_of(part * 8, 8)
        rows = lax.broadcasted_iota(jnp.int32, (8, LANES), 0) + first
        for found, low in ((near_slot, 1), (far_slot, 8)):
            which = jnp.full((8, LANES), 7, jnp.int32)
            for at in range(7):
                which = jnp.where(rows == index[low + at : low + at + 1, :], at, which)
            found[pl.ds(first, 8)] = which

    def fill_columns(a):
        columns = pl.ds(pl.multiple_of(a * LANES, LANES), LANES)
        last = lax.broadcasted_iota(jnp.int32, (8, LANES), 0) == 7
        for b in range(ORB):
            blocks = ham[a, b].astype(f32)
            itself = blocks[0:1]
            tables = []
            for low in (1, 8):
                rows = jnp.concatenate([blocks[low : low + 7], blocks[0:1]], axis=0)
                tables.append(jnp.where(last, 0.0, rows))

            def block(first, count):
                made = []
                for at in range(first, first + count, 8):
                    made.append(
                        jnp.take_along_axis(tables[0], near_slot[at : at + 8], axis=0)
                        + jnp.take_along_axis(tables[1], far_slot[at : at + 8], axis=0)
                    )
                return jnp.concatenate(made, axis=0)

            own = block(0, LANES)
            shape = (LANES, LANES)
            same = lax.broadcasted_iota(jnp.int32, shape, 0) == lax.broadcasted_iota(
                jnp.int32, shape, 1
            )
            own = jnp.where(same, itself, own)
            ht_own[b * LANES : (b + 1) * LANES, columns] = own.astype(bf16)
            for f in range(FACES):
                to = (f * ORB + b) * FACE
                made = block(LANES + f * FACE, FACE)
                ht_ghost[to : to + FACE, columns] = made.astype(bf16)
            for e in range(EDGES):
                to = e * EDGE_ROWS + b * EDGE
                small_ham[to : to + EDGE] = block(LANES + FACES * FACE + e * EDGE, EDGE)
            for side in range(2):
                to = RELAY_AT - EDGE_AT + side * RELAY_ROWS + b * RELAY
                small_ham[to : to + RELAY] = block(LANES + DIRECT + side * RELAY, RELAY)
        ht_ghost[EDGE_AT:GHOST, columns] = small_ham[...].astype(bf16)

    pl.loop(0, 5)(fill_columns)
    pass_on(0)
    pl.loop(5, ORB)(fill_columns)

    def multiply(rows, ext, operator, first, span=slice(None)):
        @pl.loop(0, 3)
        def _(part):
            columns = pl.ds(pl.multiple_of(part * SHARE, SHARE), SHARE)
            product = dot(ext[rows, span], operator[span, columns])
            if first:
                acc[rows, columns] = product
            else:
                acc[rows, columns] += product

    def multiply_ghosts(step, rows):
        if step > 0:
            pass_on(step)
        ext_ghost[rows, 0:RELAY_AT] = rbuf[step, 0:RELAY_AT].T
        multiply(rows, ext_ghost, ht_ghost, False, slice(0, RELAY_AT))
        for copy in relayed[step]:
            copy.wait_recv()
        ext_ghost[rows, RELAY_AT:GHOST] = rbuf[step, RELAY_AT:GHOST].T
        multiply(rows, ext_ghost, ht_ghost, False, slice(RELAY_AT, GHOST))

    vectors = (slice(0, HALF), slice(HALF, LANES))
    pieces = (slice(0, LANES), slice(LANES, 2 * LANES))

    def summed(half):
        base = half * LANES
        return acc[base : base + HALF] + acc[base + HALF : base + LANES]

    def send_half(order, half):
        high, low = halves(chain[order, vectors[half]])
        ext_own[half * LANES : half * LANES + HALF] = high
        ext_own[half * LANES + HALF : (half + 1) * LANES] = low
        step = 2 * order - 1 + half
        pack(
            step,
            lambda b: dot_t(picks[0:DIRECT], ext_own[pieces[half], b * LANES : (b + 1) * LANES]),
        )
        for copy in flying[step]:
            copy.start()

    multiply(pieces[0], ext_own, ht_own, True)
    multiply_ghosts(0, pieces[0])
    chain[1] = acc[0:LANES]
    send_half(1, 0)
    send_half(1, 1)
    res[...] = coef[0] * chain[0] + coef[1] * chain[1]

    for b in range(ORB):
        parts = []
        for f in range(FACES):
            at = (f * ORB + b) * FACE
            parts.append(rbuf[0, at : at + FACE])
        noise_rows = jnp.concatenate(parts, axis=0)
        noise_ext[b * LANES : (b + 1) * LANES, LANES : LANES + FACES * FACE] = noise_rows.T
    small_ghost = rbuf[0, EDGE_AT:GHOST].astype(f32)
    for b in range(ORB):
        parts = []
        for e in range(EDGES):
            at = e * EDGE_ROWS + b * EDGE
            parts.append(small_ghost[at : at + EDGE])
        for side in range(2):
            at = RELAY_AT - EDGE_AT + side * RELAY_ROWS + b * RELAY
            parts.append(small_ghost[at : at + RELAY])
        parts.append(jnp.zeros((EXT - LANES - PICKED, LANES), f32))
        noise_rows = jnp.concatenate(parts, axis=0).astype(bf16)
        noise_ext[b * LANES : (b + 1) * LANES, LANES + FACES * FACE : EXT] = noise_rows.T

    multiply(slice(0, 2 * LANES), ext_own, ht_own, True)

    @pl.loop(0, (NEIGH - 1) // 2)
    def _(two):
        hot = onehot[:, pl.ds(pl.multiple_of(two * 2 * LANES + LANES, LANES), 2 * LANES)]
        both = dot(noise_ext[...], hot).astype(bf16)
        gathered[2 * two] = both[:, 0:LANES]
        gathered[2 * two + 1] = both[:, LANES:]

    for half in range(2):
        multiply_ghosts(1 + half, pieces[half])
        chain[2, vectors[half]] = 2.0 * summed(half) - chain[0, vectors[half]]
        send_half(2, half)
        multiply(pieces[half], ext_own, ht_own, True)
    res[...] += coef[2] * chain[2]

    dens[:, 0:1] = jnp.zeros((ORB * ORB, 1, LANES), f32)

    for half in range(2):
        multiply_ghosts(3 + half, pieces[half])
        res[vectors[half]] += coef[3] * (2.0 * summed(half) - chain[1, vectors[half]])

        @pl.loop(1, NEIGH)
        def _(m):
            for b in range(ORB):
                base = b * LANES + half * HALF
                near = gathered[m - 1, base : base + HALF].astype(f32)
                for a in range(ORB):
                    term = res[vectors[half], a * LANES : (a + 1) * LANES] * near
                    row = jnp.sum(term, axis=0, keepdims=True)
                    if half == 0:
                        dens[a * ORB + b, pl.ds(m, 1)] = row
                    else:
                        dens[a * ORB + b, pl.ds(m, 1)] += row

    pairs[...] = jnp.zeros(pairs.shape, f32)
    for c in range(3):
        def add(ab, total):
            return total + deriv[c, ab].astype(f32) * dens[ab, 0:NEIGH]

        total = lax.fori_loop(0, ORB * ORB, add, jnp.zeros((NEIGH, LANES), f32), unroll=9)
        pair = total * (1.0 / LANES)
        pairs[c : c + 1, 0:LANES] = -jnp.sum(pair, axis=0, keepdims=True)
        for m in range(1, NEIGH):
            pairs[c : c + 1, m * LANES : (m + 1) * LANES] = pair[m : m + 1]
    high, low = halves(pairs[...])
    spread = dot_t(jnp.concatenate([high, low], axis=0), onehot[...])
    spread = spread[0:8] + spread[8:16]
    high, low = halves(spread[:, LANES:EXT])
    mask = spans[...]
    shape = (COPIES * 8, SHARE)
    high = (high.astype(f32)[None] * mask).reshape(shape).astype(bf16)
    low = (low.astype(f32)[None] * mask).reshape(shape).astype(bf16)
    tiles = dot(high[:, 0:PICKED], picks[...]) + dot(low[:, 0:PICKED], picks[...])
    fsend[...] = tiles.reshape(COPIES, 8, LANES)

    back = []
    for at, (direction, _, _) in enumerate(SEGMENTS):
        back.append(
            pltpu.make_async_remote_copy(
                src_ref=fsend.at[at],
                dst_ref=frecv.at[at],
                send_sem=send_sem.at[5, at],
                recv_sem=recv_sem.at[5, at],
                device_id=shifted(direction, 1),
                device_id_type=MESH,
            )
        )
    for copy in back:
        copy.start()
    for a in range(ORB):
        w_out[a] = res[:, a * LANES : (a + 1) * LANES].T
    for copy in back:
        copy.wait_recv()
    total = spread[:, 0:LANES]
    for at in range(COPIES):
        total = total + frecv[at]
    f_out[...] = total[0:3]
    for group in flying + relayed:
        for copy in group:
            copy.wait_send()
    for copy in back:
        copy.wait_send()


def extended_slots(sizes, neighbours):
    atom_count = neighbours.shape[0]
    cell_count = CX * CY * CZ
    size_x, size_y, size_z = sizes
    ids = neighbours.T
    domain = ids // atom_count
    within = ids % atom_count
    basis = within // cell_count
    remain = within % cell_count
    parts = (
        (domain // (size_y * size_z), remain // (CY * CZ), "gx", CX, size_x),
        (domain // size_z % size_y, remain // CZ % CY, "gy", CY, size_y),
        (domain % size_z, remain % CZ, "gz", CZ, size_z),
    )
    signs = []
    inside = basis
    for dom, cell, axis, cells, size in parts:
        place = jnp.remainder((dom - lax.axis_index(axis)) * cells + cell + 1, cells * size)
        sign = jnp.where(place == 0, -1, jnp.where(place == cells + 1, 1, 0))
        signs.append(sign)
        inside = jnp.where(sign == 0, inside * cells + place - 1, inside)
    code = signs[0] * 9 + signs[1] * 3 + signs[2]
    first = jnp.zeros_like(code)
    for (dx, dy, dz), row, _ in SEGMENTS:
        first = jnp.where(code == dx * 9 + dy * 3 + dz, LANES + row, first)
    return first + inside


def shards(sizes, noise, ham, deriv, neighbours, coef):
    f32 = jnp.float32
    bf16 = jnp.bfloat16
    index = extended_slots(sizes, neighbours)
    ham = ham.transpose(1, 2, 0, 3)
    deriv = deriv.transpose(0, 2, 3, 1, 4).reshape(3, ORB * ORB, NEIGH, LANES)
    picks = jnp.asarray(picking_matrix(), bf16)
    relays = jnp.asarray(relaying_matrix(), bf16)
    spans = jnp.asarray(segment_spans(), f32)
    vmem = pl.BlockSpec(memory_space=pltpu.VMEM)
    smem = pl.BlockSpec(memory_space=pltpu.SMEM)
    return pl.pallas_call(
        functools.partial(kernel, sizes),
        out_shape=(
            jax.ShapeDtypeStruct((ORB, LANES, LANES), f32),
            jax.ShapeDtypeStruct((3, LANES), f32),
        ),
        in_specs=[vmem, vmem, vmem, vmem, smem, vmem, vmem, vmem],
        out_specs=(vmem, vmem),
        scratch_shapes=[
            pltpu.VMEM((WIDE, WIDE), bf16),
            pltpu.VMEM((GHOST, WIDE), bf16),
            pltpu.VMEM((EXT, NEIGH * LANES), bf16),
            pltpu.VMEM((2 * LANES, WIDE), bf16),
            pltpu.VMEM((2 * LANES, GHOST), bf16),
            pltpu.VMEM((WIDE, EXT), bf16),
            pltpu.VMEM((NEIGH - 1, WIDE, LANES), bf16),
            pltpu.VMEM((3, LANES, WIDE), f32),
            pltpu.VMEM((LANES, WIDE), f32),
            pltpu.VMEM((2 * LANES, WIDE), f32),
            pltpu.VMEM((5, SENT, LANES), bf16),
            pltpu.VMEM((5, GHOST, LANES), bf16),
            pltpu.VMEM((EDGES * EDGE_ROWS, LANES), f32),
            pltpu.VMEM((SMALL, LANES), f32),
            pltpu.VMEM((2 * RELAY_ROWS, LANES), f32),
            pltpu.VMEM((LANES + PICKED, LANES), jnp.int32),
            pltpu.VMEM((LANES + PICKED, LANES), jnp.int32),
            pltpu.VMEM((COPIES, 8, LANES), f32),
            pltpu.VMEM((COPIES, 8, LANES), f32),
            pltpu.VMEM((8, NEIGH * LANES), f32),
            pltpu.VMEM((ORB * ORB, 16, LANES), f32),
            pltpu.SemaphoreType.DMA((6, COPIES)),
            pltpu.SemaphoreType.DMA((6, COPIES)),
        ],
        compiler_params=pltpu.CompilerParams(
            collective_id=0, has_side_effects=True, vmem_limit_bytes=56 * 1024 * 1024
        ),
        name="fermi_forces",
    )(noise, ham, deriv, index, coef, picks, relays, spans)


def solution(mesh):
    sizes = tuple(mesh.shape[name] for name in ("gx", "gy", "gz"))
    in_specs = (
        P(None, ("gx", "gy", "gz"), None),
        P(None, None, None, ("gx", "gy", "gz")),
        P(None, None, None, None, ("gx", "gy", "gz")),
        P(("gx", "gy", "gz"), None),
        P(),
    )
    out_specs = (P(None, ("gx", "gy", "gz"), None), P(None, ("gx", "gy", "gz")))
    return jax.shard_map(
        functools.partial(shards, sizes),
        mesh=mesh,
        in_specs=in_specs,
        out_specs=out_specs,
        check_vma=False,
    )
```

```python
import functools

import jax
import jax.numpy as jnp
import numpy as np
from jax import lax
from jax.experimental import pallas as pl
from jax.experimental.pallas import tpu as pltpu
from jax.sharding import PartitionSpec as P

MESH = pl.DeviceIdType.MESH
CX = 4
CY = 4
CZ = 4
NEIGH = 15
ORB = 9
LANES = 128
HALF = 64
WIDE = ORB * LANES
FACE = 32
EDGE = 8
CORNER = 2
FACES = 6
EDGES = 4
DIRECT = FACES * FACE + EDGES * EDGE
RELAY = 4 * EDGE + 4 * CORNER
PICKED = DIRECT + 2 * RELAY
EXT = 512
FACE_ROWS = ORB * FACE
EDGE_ROWS = 80
RELAY_ROWS = 368
EDGE_AT = FACES * FACE_ROWS
RELAY_AT = EDGE_AT + EDGES * EDGE_ROWS
SENT = RELAY_AT + 2 * RELAY_ROWS
GHOST = SENT + 32
SHARE = 384
COLUMNS = WIDE + GHOST
NONE = LANES - 1
HELD = ((-1, 0, 0), (1, 0, 0), (0, 0, -1), (0, 0, 1), (-1, 0, -1), (-1, 0, 1), (1, 0, -1), (1, 0, 1))


def ghost_segments():
    order = HELD[0:4] + ((0, -1, 0), (0, 1, 0)) + HELD[4:8]
    for dy in (-1, 1):
        order = order + tuple((dx, dy, dz) for dx, _, dz in HELD)
    placed = []
    first = 0
    for direction in order:
        placed.append((direction, first, atoms_in(direction)))
        first += atoms_in(direction)
    return placed


def atoms_in(direction):
    return (FACE, EDGE, CORNER)[sum(abs(d) for d in direction) - 1]


SEGMENTS = ghost_segments()
COPIES = len(SEGMENTS)


def cells_of(d, cells):
    return range(cells) if d == 0 else ((0,) if d > 0 else (cells - 1,))


def picking_matrix():
    picks = np.zeros((PICKED, LANES), np.float32)
    row = 0
    for (dx, dy, dz), _, _ in SEGMENTS:
        for basis in range(2):
            for x in cells_of(dx, CX):
                for y in cells_of(dy, CY):
                    for z in cells_of(dz, CZ):
                        picks[row, ((basis * CX + x) * CY + y) * CZ + z] = 1.0
                        row += 1
    return picks


def relaying_matrix():
    picks = np.zeros((2 * RELAY, 4 * FACE + 4 * EDGE), np.float32)
    row = 0
    for dy in (-1, 1):
        held = 0
        for dx, _, dz in HELD:
            for basis in range(2):
                for x in cells_of(dx, CX):
                    for y in range(CY):
                        for z in cells_of(dz, CZ):
                            if y in cells_of(dy, CY):
                                picks[row, held] = 1.0
                                row += 1
                            held += 1
    return picks


def column_slots():
    slots = np.full((1, COLUMNS), -1.0, np.float32)
    orbitals = np.zeros((1, COLUMNS), np.int32)
    for b in range(ORB):
        slots[0, b * LANES : (b + 1) * LANES] = np.arange(LANES)
        orbitals[0, b * LANES : (b + 1) * LANES] = b
        for f in range(FACES):
            at = WIDE + (f * ORB + b) * FACE
            slots[0, at : at + FACE] = LANES + f * FACE + np.arange(FACE)
            orbitals[0, at : at + FACE] = b
        for e in range(EDGES):
            at = WIDE + EDGE_AT + e * EDGE_ROWS + b * EDGE
            slots[0, at : at + EDGE] = LANES + FACES * FACE + e * EDGE + np.arange(EDGE)
            orbitals[0, at : at + EDGE] = b
        for side in range(2):
            at = WIDE + RELAY_AT + side * RELAY_ROWS + b * RELAY
            slots[0, at : at + RELAY] = LANES + DIRECT + side * RELAY + np.arange(RELAY)
            orbitals[0, at : at + RELAY] = b
    return slots, orbitals * (NEIGH - 1)


def segment_spans():
    spans = np.zeros((COPIES, 8, SHARE), np.float32)
    for at, (_, first, count) in enumerate(SEGMENTS):
        spans[at, :, first : first + count] = 1.0
    return spans


def dot(a, b):
    return jnp.dot(a, b, preferred_element_type=jnp.float32)


def dot_t(a, b):
    return lax.dot_general(a, b, (((1,), (1,)), ((), ())), preferred_element_type=jnp.float32)


def halves(x):
    high = x.astype(jnp.bfloat16)
    return high, (x - high.astype(jnp.float32)).astype(jnp.bfloat16)


def kernel(
    sizes,
    noise,
    ham,
    deriv,
    index,
    coef,
    picks,
    relays,
    spans,
    column_slot,
    column_base,
    w_out,
    f_out,
    operator,
    lookup,
    table,
    onehot,
    ext_own,
    noise_ext,
    gathered,
    chain,
    res,
    res_t,
    acc,
    sbuf,
    rbuf,
    small,
    small_relay,
    fsend,
    frecv,
    pairs,
    dens,
    send_sem,
    recv_sem,
):
    f32 = jnp.float32
    bf16 = jnp.bfloat16
    here = [lax.axis_index(name) for name in ("gx", "gy", "gz")]

    def shifted(direction, sign):
        return tuple(
            lax.rem(me + size + sign * d, size) for me, size, d in zip(here, sizes, direction)
        )

    barrier = pltpu.get_barrier_semaphore()
    for direction, _, _ in SEGMENTS:
        pl.semaphore_signal(barrier, inc=1, device_id=shifted(direction, -1), device_id_type=MESH)

    def pack(step, rows_of):
        for b in range(ORB):
            rows = rows_of(b)
            for f in range(FACES):
                to = (f * ORB + b) * FACE
                sbuf[step, to : to + FACE] = rows[f * FACE : (f + 1) * FACE].astype(bf16)
            for e in range(EDGES):
                at = FACES * FACE + e * EDGE
                to = e * EDGE_ROWS + b * EDGE
                small[to : to + EDGE] = rows[at : at + EDGE]
        sbuf[step, EDGE_AT:RELAY_AT] = small[0 : EDGES * EDGE_ROWS].astype(bf16)

    def copy_rows(step, at, first, rows, direction):
        return pltpu.make_async_remote_copy(
            src_ref=sbuf.at[step, pl.ds(first, rows), :],
            dst_ref=rbuf.at[step, pl.ds(first, rows), :],
            send_sem=send_sem.at[step, at],
            recv_sem=recv_sem.at[step, at],
            device_id=shifted(direction, -1),
            device_id_type=MESH,
        )

    def copies(step):
        made = []
        for at, (direction, _, _) in enumerate(SEGMENTS[0 : FACES + EDGES]):
            if at < FACES:
                made.append(copy_rows(step, at, at * FACE_ROWS, FACE_ROWS, direction))
            else:
                first = EDGE_AT + (at - FACES) * EDGE_ROWS
                made.append(copy_rows(step, at, first, EDGE_ROWS, direction))
        return made

    def relay_copies(step):
        made = []
        for at, dy in enumerate((-1, 1)):
            first = RELAY_AT + at * RELAY_ROWS
            made.append(copy_rows(step, FACES + EDGES + at, first, RELAY_ROWS, (0, dy, 0)))
        return made

    flying = [copies(step) for step in range(5)]
    relayed = [relay_copies(step) for step in range(5)]

    def pass_on(step):
        for copy in flying[step]:
            copy.wait_recv()
        edges = rbuf[step, EDGE_AT:RELAY_AT].astype(f32)
        for b in range(ORB):
            parts = []
            for f in range(4):
                at = (f * ORB + b) * FACE
                parts.append(rbuf[step, at : at + FACE])
            lines = []
            for e in range(EDGES):
                at = e * EDGE_ROWS + b * EDGE
                lines.append(edges[at : at + EDGE])
            parts.append(jnp.concatenate(lines, axis=0).astype(bf16))
            rows = dot(relays[...], jnp.concatenate(parts, axis=0))
            for side in range(2):
                to = side * RELAY_ROWS + b * RELAY
                small_relay[to : to + RELAY] = rows[side * RELAY : (side + 1) * RELAY]
        sbuf[step, RELAY_AT:SENT] = small_relay[...].astype(bf16)
        for copy in relayed[step]:
            copy.start()

    small[...] = jnp.zeros(small.shape, f32)
    small_relay[...] = jnp.zeros(small_relay.shape, f32)
    for step in range(5):
        rbuf[step, SENT:GHOST] = jnp.zeros((GHOST - SENT, LANES), bf16)
    pack(0, lambda b: dot(picks[0:DIRECT], noise[b]))
    pl.semaphore_wait(barrier, COPIES)
    for copy in flying[0]:
        copy.start()

    @pl.loop(0, EXT // LANES)
    def _(part):
        first = pl.multiple_of(part * LANES, LANES)
        rows = lax.broadcasted_iota(jnp.int32, (LANES, LANES), 0) + first
        for m in range(NEIGH):
            same = rows == index[m : m + 1, :]
            onehot[pl.ds(first, LANES), m * LANES : (m + 1) * LANES] = jnp.where(
                same, 1.0, 0.0
            ).astype(bf16)

    turned = jnp.concatenate([index[...], index[0:1]], axis=0).astype(f32).T
    res[0:LANES, 0:16] = turned

    @pl.loop(0, LANES // 8)
    def _(part):
        lines = pl.ds(pl.multiple_of(part * 8, 8), 8)
        near = res[lines, 0:16]
        near = [jnp.broadcast_to(near[:, m : m + 1], (8, LANES)) for m in range(1, NEIGH)]
        own = None
        for tile in range(COLUMNS // LANES):
            cut = slice(tile * LANES, (tile + 1) * LANES)
            base = column_base[0:1, cut]
            if 0 < tile < ORB:
                which = jnp.where(own == NONE, NONE, own + tile * (NEIGH - 1))
            else:
                slot = column_slot[0:1, cut]
                which = jnp.full((8, LANES), NONE, jnp.int32)
                for m in range(NEIGH - 1):
                    which = jnp.where(near[m] == slot, base + m, which)
                if tile == 0:
                    own = which
            lookup[lines, cut] = which

    def fill_rows(a):
        blocks = [ham[a, b].astype(f32) for b in range(ORB)]
        lines = [block[1:NEIGH] for block in blocks]
        lines.append(jnp.zeros((LANES - ORB * (NEIGH - 1), LANES), f32))
        table[:, 0:LANES] = jnp.concatenate(lines, axis=0).T
        firsts = [block[0:1] for block in blocks] + [jnp.zeros((16 - ORB, LANES), f32)]
        table[:, LANES : LANES + 16] = jnp.concatenate(firsts, axis=0).T
        shape = (8, LANES)
        for pair in range(LANES // 16):
            at = pl.multiple_of(a * LANES + pair * 16, 16)
            for tile in range(COLUMNS // LANES):
                cut = slice(tile * LANES, (tile + 1) * LANES)
                made = []
                for low in (pair * 16, pair * 16 + 8):
                    found = jnp.take_along_axis(
                        table[low : low + 8, 0:LANES], lookup[low : low + 8, cut], axis=1
                    )
                    if tile < ORB:
                        itself = table[low : low + 8, LANES + tile : LANES + tile + 1]
                        same = lax.broadcasted_iota(jnp.int32, shape, 0) + low
                        same = same == lax.broadcasted_iota(jnp.int32, shape, 1)
                        found = jnp.where(same, itself, found)
                    made.append(found)
                operator[pl.ds(at, 16), cut] = jnp.concatenate(made, axis=0).astype(bf16)

    pl.loop(0, 5)(fill_rows)
    pass_on(0)
    pl.loop(5, ORB)(fill_rows)

    own_columns = slice(0, WIDE)
    direct_columns = slice(WIDE, WIDE + RELAY_AT)
    relay_columns = slice(WIDE + RELAY_AT, COLUMNS)

    def multiply_ghosts(step, half):
        if step > 0:
            pass_on(step)
        acc[half] += dot(operator[:, direct_columns], rbuf[step, 0:RELAY_AT])
        for copy in relayed[step]:
            copy.wait_recv()
        acc[half] += dot(operator[:, relay_columns], rbuf[step, RELAY_AT:GHOST])

    left = lax.broadcasted_iota(jnp.int32, (WIDE, LANES), 1) < HALF

    def summed(half):
        return acc[half] + pltpu.roll(acc[half], HALF, 1)

    def send_half(order, half):
        value = chain[order]
        high = value.astype(bf16).astype(f32)
        low = value - high
        if half == 0:
            both = jnp.where(left, high, pltpu.roll(low, HALF, 1))
        else:
            both = jnp.where(left, pltpu.roll(high, HALF, 1), low)
        ext_own[:, half * LANES : (half + 1) * LANES] = both.astype(bf16)
        step = 2 * order - 1 + half
        pack(
            step,
            lambda b: dot(
                picks[0:DIRECT],
                ext_own[b * LANES : (b + 1) * LANES, half * LANES : (half + 1) * LANES],
            ),
        )
        for copy in flying[step]:
            copy.start()

    for b in range(ORB):
        chain[0, b * LANES : (b + 1) * LANES] = noise[b].astype(f32)
        ext_own[b * LANES : (b + 1) * LANES, 0:LANES] = noise[b]
    acc[0] = dot(operator[:, own_columns], ext_own[:, 0:LANES])
    multiply_ghosts(0, 0)
    chain[1] = acc[0]
    send_half(1, 0)
    send_half(1, 1)
    res[...] = coef[0] * chain[0] + coef[1] * chain[1]

    both = dot(operator[:, own_columns], ext_own[...])
    acc[0] = both[:, 0:LANES]
    acc[1] = both[:, LANES:]
    small_ghost = rbuf[0, EDGE_AT:GHOST].astype(f32)
    for b in range(ORB):
        parts = []
        for f in range(FACES):
            at = (f * ORB + b) * FACE
            parts.append(rbuf[0, at : at + FACE])
        lines = []
        for e in range(EDGES):
            at = e * EDGE_ROWS + b * EDGE
            lines.append(small_ghost[at : at + EDGE])
        for side in range(2):
            at = RELAY_AT - EDGE_AT + side * RELAY_ROWS + b * RELAY
            lines.append(small_ghost[at : at + RELAY])
        lines.append(jnp.zeros((EXT - LANES - PICKED, LANES), f32))
        parts.append(jnp.concatenate(lines, axis=0).astype(bf16))
        cut = slice(b * LANES, (b + 1) * LANES)
        noise_ext[cut, 0:LANES] = noise[b].T
        noise_ext[cut, LANES:EXT] = jnp.concatenate(parts, axis=0).T

    @pl.loop(0, (NEIGH - 1) // 2)
    def _(two):
        hot = onehot[:, pl.ds(pl.multiple_of(two * 2 * LANES + LANES, LANES), 2 * LANES)]
        both = dot(noise_ext[...], hot).astype(bf16)
        gathered[2 * two] = both[:, 0:LANES]
        gathered[2 * two + 1] = both[:, LANES:]

    for half in range(2):
        multiply_ghosts(1 + half, half)
        fresh = 2.0 * summed(half) - chain[0]
        chain[2] = fresh if half == 0 else jnp.where(left, chain[2], fresh)
        send_half(2, half)
        cut = slice(half * LANES, (half + 1) * LANES)
        acc[half] = dot(operator[:, own_columns], ext_own[:, cut])
    res[...] += coef[2] * chain[2]

    dens[:, 0:1] = jnp.zeros((ORB * ORB, 1, LANES), f32)

    for half in range(2):
        multiply_ghosts(3 + half, half)
        fresh = coef[3] * (2.0 * summed(half) - chain[1])
        res[...] += jnp.where(left, fresh, 0.0) if half == 0 else jnp.where(left, 0.0, fresh)
        for a in range(ORB):
            res_t[a] = res[a * LANES : (a + 1) * LANES].T

        @pl.loop(1, NEIGH)
        def _(m):
            for b in range(ORB):
                base = b * LANES + half * HALF
                near = gathered[m - 1, base : base + HALF].astype(f32)
                for a in range(ORB):
                    term = res_t[a, half * HALF : (half + 1) * HALF] * near
                    row = jnp.sum(term, axis=0, keepdims=True)
                    if half == 0:
                        dens[a * ORB + b, pl.ds(m, 1)] = row
                    else:
                        dens[a * ORB + b, pl.ds(m, 1)] += row

    pairs[...] = jnp.zeros(pairs.shape, f32)
    for c in range(3):
        def add(ab, total):
            return total + deriv[c, ab].astype(f32) * dens[ab, 0:NEIGH]

        total = lax.fori_loop(0, ORB * ORB, add, jnp.zeros((NEIGH, LANES), f32), unroll=9)
        pair = total * (1.0 / LANES)
        pairs[c : c + 1, 0:LANES] = -jnp.sum(pair, axis=0, keepdims=True)
        for m in range(1, NEIGH):
            pairs[c : c + 1, m * LANES : (m + 1) * LANES] = pair[m : m + 1]
    high, low = halves(pairs[...])
    spread = dot_t(jnp.concatenate([high, low], axis=0), onehot[...])
    spread = spread[0:8] + spread[8:16]
    high, low = halves(spread[:, LANES:EXT])
    mask = spans[...]
    shape = (COPIES * 8, SHARE)
    high = (high.astype(f32)[None] * mask).reshape(shape).astype(bf16)
    low = (low.astype(f32)[None] * mask).reshape(shape).astype(bf16)
    tiles = dot(high[:, 0:PICKED], picks[...]) + dot(low[:, 0:PICKED], picks[...])
    fsend[...] = tiles.reshape(COPIES, 8, LANES)

    back = []
    for at, (direction, _, _) in enumerate(SEGMENTS):
        back.append(
            pltpu.make_async_remote_copy(
                src_ref=fsend.at[at],
                dst_ref=frecv.at[at],
                send_sem=send_sem.at[5, at],
                recv_sem=recv_sem.at[5, at],
                device_id=shifted(direction, 1),
                device_id_type=MESH,
            )
        )
    for copy in back:
        copy.start()
    for a in range(ORB):
        w_out[a] = res[a * LANES : (a + 1) * LANES]
    for copy in back:
        copy.wait_recv()
    total = spread[:, 0:LANES]
    for at in range(COPIES):
        total = total + frecv[at]
    f_out[...] = total[0:3]
    for group in flying + relayed:
        for copy in group:
            copy.wait_send()
    for copy in back:
        copy.wait_send()


def extended_slots(sizes, neighbours):
    atom_count = neighbours.shape[0]
    cell_count = CX * CY * CZ
    size_x, size_y, size_z = sizes
    ids = neighbours.T
    domain = ids // atom_count
    within = ids % atom_count
    basis = within // cell_count
    remain = within % cell_count
    parts = (
        (domain // (size_y * size_z), remain // (CY * CZ), "gx", CX, size_x),
        (domain // size_z % size_y, remain // CZ % CY, "gy", CY, size_y),
        (domain % size_z, remain % CZ, "gz", CZ, size_z),
    )
    signs = []
    inside = basis
    for dom, cell, axis, cells, size in parts:
        place = jnp.remainder((dom - lax.axis_index(axis)) * cells + cell + 1, cells * size)
        sign = jnp.where(place == 0, -1, jnp.where(place == cells + 1, 1, 0))
        signs.append(sign)
        inside = jnp.where(sign == 0, inside * cells + place - 1, inside)
    code = signs[0] * 9 + signs[1] * 3 + signs[2]
    first = jnp.zeros_like(code)
    for (dx, dy, dz), row, _ in SEGMENTS:
        first = jnp.where(code == dx * 9 + dy * 3 + dz, LANES + row, first)
    return first + inside


def shards(sizes, noise, ham, deriv, neighbours, coef):
    f32 = jnp.float32
    bf16 = jnp.bfloat16
    index = extended_slots(sizes, neighbours)
    ham = ham.transpose(1, 2, 0, 3)
    deriv = deriv.transpose(0, 2, 3, 1, 4).reshape(3, ORB * ORB, NEIGH, LANES)
    picks = jnp.asarray(picking_matrix(), bf16)
    relays = jnp.asarray(relaying_matrix(), bf16)
    spans = jnp.asarray(segment_spans(), f32)
    column_slot, column_base = (jnp.asarray(value) for value in column_slots())
    vmem = pl.BlockSpec(memory_space=pltpu.VMEM)
    smem = pl.BlockSpec(memory_space=pltpu.SMEM)
    return pl.pallas_call(
        functools.partial(kernel, sizes),
        out_shape=(
            jax.ShapeDtypeStruct((ORB, LANES, LANES), f32),
            jax.ShapeDtypeStruct((3, LANES), f32),
        ),
        in_specs=[vmem, vmem, vmem, vmem, smem, vmem, vmem, vmem, vmem, vmem],
        out_specs=(vmem, vmem),
        scratch_shapes=[
            pltpu.VMEM((WIDE, COLUMNS), bf16),
            pltpu.VMEM((LANES, COLUMNS), jnp.int32),
            pltpu.VMEM((LANES, 2 * LANES), f32),
            pltpu.VMEM((EXT, NEIGH * LANES), bf16),
            pltpu.VMEM((WIDE, 2 * LANES), bf16),
            pltpu.VMEM((WIDE, EXT), bf16),
            pltpu.VMEM((NEIGH - 1, WIDE, LANES), bf16),
            pltpu.VMEM((3, WIDE, LANES), f32),
            pltpu.VMEM((WIDE, LANES), f32),
            pltpu.VMEM((ORB, LANES, LANES), f32),
            pltpu.VMEM((2, WIDE, LANES), f32),
            pltpu.VMEM((5, SENT, LANES), bf16),
            pltpu.VMEM((5, GHOST, LANES), bf16),
            pltpu.VMEM((EDGES * EDGE_ROWS, LANES), f32),
            pltpu.VMEM((2 * RELAY_ROWS, LANES), f32),
            pltpu.VMEM((COPIES, 8, LANES), f32),
            pltpu.VMEM((COPIES, 8, LANES), f32),
            pltpu.VMEM((8, NEIGH * LANES), f32),
            pltpu.VMEM((ORB * ORB, 16, LANES), f32),
            pltpu.SemaphoreType.DMA((6, COPIES)),
            pltpu.SemaphoreType.DMA((6, COPIES)),
        ],
        compiler_params=pltpu.CompilerParams(
            collective_id=0, has_side_effects=True, vmem_limit_bytes=56 * 1024 * 1024
        ),
        name="fermi_forces",
    )(noise, ham, deriv, index, coef, picks, relays, spans, column_slot, column_base)


def solution(mesh):
    sizes = tuple(mesh.shape[name] for name in ("gx", "gy", "gz"))
    in_specs = (
        P(None, ("gx", "gy", "gz"), None),
        P(None, None, None, ("gx", "gy", "gz")),
        P(None, None, None, None, ("gx", "gy", "gz")),
        P(("gx", "gy", "gz"), None),
        P(),
    )
    out_specs = (P(None, ("gx", "gy", "gz"), None), P(None, ("gx", "gy", "gz")))
    return jax.shard_map(
        functools.partial(shards, sizes),
        mesh=mesh,
        in_specs=in_specs,
        out_specs=out_specs,
        check_vma=False,
    )
```

```python
import functools

import jax
import jax.numpy as jnp
import numpy as np
from jax import lax
from jax.experimental import pallas as pl
from jax.experimental.pallas import tpu as pltpu
from jax.sharding import PartitionSpec as P

MESH = pl.DeviceIdType.MESH
CX = 4
CY = 4
CZ = 4
NEIGH = 15
ORB = 9
LANES = 128
HALF = 64
WIDE = ORB * LANES
FACE = 32
EDGE = 8
CORNER = 2
FACES = 6
EDGES = 4
DIRECT = FACES * FACE + EDGES * EDGE
RELAY = 4 * EDGE + 4 * CORNER
PICKED = DIRECT + 2 * RELAY
EXT = 512
FACE_ROWS = ORB * FACE
EDGE_ROWS = 80
RELAY_ROWS = 368
EDGE_AT = FACES * FACE_ROWS
RELAY_AT = EDGE_AT + EDGES * EDGE_ROWS
SENT = RELAY_AT + 2 * RELAY_ROWS
GHOST = SENT + 32
SMALL = GHOST - EDGE_AT
SHARE = 384
HELD = ((-1, 0, 0), (1, 0, 0), (0, 0, -1), (0, 0, 1), (-1, 0, -1), (-1, 0, 1), (1, 0, -1), (1, 0, 1))


def ghost_segments():
    order = HELD[0:4] + ((0, -1, 0), (0, 1, 0)) + HELD[4:8]
    for dy in (-1, 1):
        order = order + tuple((dx, dy, dz) for dx, _, dz in HELD)
    placed = []
    first = 0
    for direction in order:
        placed.append((direction, first, atoms_in(direction)))
        first += atoms_in(direction)
    return placed


def atoms_in(direction):
    return (FACE, EDGE, CORNER)[sum(abs(d) for d in direction) - 1]


SEGMENTS = ghost_segments()
COPIES = len(SEGMENTS)


def cells_of(d, cells):
    return range(cells) if d == 0 else ((0,) if d > 0 else (cells - 1,))


def picking_matrix():
    picks = np.zeros((PICKED, LANES), np.float32)
    row = 0
    for (dx, dy, dz), _, _ in SEGMENTS:
        for basis in range(2):
            for x in cells_of(dx, CX):
                for y in cells_of(dy, CY):
                    for z in cells_of(dz, CZ):
                        picks[row, ((basis * CX + x) * CY + y) * CZ + z] = 1.0
                        row += 1
    return picks


def relaying_matrix():
    picks = np.zeros((2 * RELAY, 4 * FACE + 4 * EDGE), np.float32)
    row = 0
    for dy in (-1, 1):
        held = 0
        for dx, _, dz in HELD:
            for basis in range(2):
                for x in cells_of(dx, CX):
                    for y in range(CY):
                        for z in cells_of(dz, CZ):
                            if y in cells_of(dy, CY):
                                picks[row, held] = 1.0
                                row += 1
                            held += 1
    return picks


def segment_spans():
    spans = np.zeros((COPIES, 8, SHARE), np.float32)
    for at, (_, first, count) in enumerate(SEGMENTS):
        spans[at, :, first : first + count] = 1.0
    return spans


def dot(a, b):
    return jnp.dot(a, b, preferred_element_type=jnp.float32)


def dot_t(a, b):
    return lax.dot_general(a, b, (((1,), (1,)), ((), ())), preferred_element_type=jnp.float32)


def halves(x):
    high = x.astype(jnp.bfloat16)
    return high, (x - high.astype(jnp.float32)).astype(jnp.bfloat16)


def kernel(
    sizes,
    noise,
    ham,
    deriv,
    index,
    coef,
    picks,
    relays,
    spans,
    w_out,
    f_out,
    ht_own,
    ht_ghost,
    onehot,
    ext_own,
    ext_ghost,
    noise_ext,
    gathered,
    chain,
    res,
    acc,
    sbuf,
    rbuf,
    small,
    small_ham,
    small_relay,
    near_slot,
    far_slot,
    fsend,
    frecv,
    pairs,
    dens,
    send_sem,
    recv_sem,
):
    f32 = jnp.float32
    bf16 = jnp.bfloat16
    here = [lax.axis_index(name) for name in ("gx", "gy", "gz")]

    def shifted(direction, sign):
        return tuple(
            lax.rem(me + size + sign * d, size) for me, size, d in zip(here, sizes, direction)
        )

    barrier = pltpu.get_barrier_semaphore()
    for direction, _, _ in SEGMENTS:
        pl.semaphore_signal(barrier, inc=1, device_id=shifted(direction, -1), device_id_type=MESH)

    def pack(step, rows_of):
        for b in range(ORB):
            rows = rows_of(b)
            for f in range(FACES):
                to = (f * ORB + b) * FACE
                sbuf[step, to : to + FACE] = rows[f * FACE : (f + 1) * FACE].astype(bf16)
            for e in range(EDGES):
                at = FACES * FACE + e * EDGE
                to = e * EDGE_ROWS + b * EDGE
                small[to : to + EDGE] = rows[at : at + EDGE]
        sbuf[step, EDGE_AT:RELAY_AT] = small[0 : EDGES * EDGE_ROWS].astype(bf16)

    def copy_rows(step, at, first, rows, direction):
        return pltpu.make_async_remote_copy(
            src_ref=sbuf.at[step, pl.ds(first, rows), :],
            dst_ref=rbuf.at[step, pl.ds(first, rows), :],
            send_sem=send_sem.at[step, at],
            recv_sem=recv_sem.at[step, at],
            device_id=shifted(direction, -1),
            device_id_type=MESH,
        )

    def copies(step):
        made = []
        for at, (direction, _, _) in enumerate(SEGMENTS[0 : FACES + EDGES]):
            if at < FACES:
                made.append(copy_rows(step, at, at * FACE_ROWS, FACE_ROWS, direction))
            else:
                first = EDGE_AT + (at - FACES) * EDGE_ROWS
                made.append(copy_rows(step, at, first, EDGE_ROWS, direction))
        return made

    def relay_copies(step):
        made = []
        for at, dy in enumerate((-1, 1)):
            first = RELAY_AT + at * RELAY_ROWS
            made.append(copy_rows(step, FACES + EDGES + at, first, RELAY_ROWS, (0, dy, 0)))
        return made

    flying = [copies(step) for step in range(5)]
    relayed = [relay_copies(step) for step in range(5)]

    def pass_on(step):
        for copy in flying[step]:
            copy.wait_recv()
        edges = rbuf[step, EDGE_AT:RELAY_AT].astype(f32)
        for b in range(ORB):
            parts = []
            for f in range(4):
                at = (f * ORB + b) * FACE
                parts.append(rbuf[step, at : at + FACE])
            lines = []
            for e in range(EDGES):
                at = e * EDGE_ROWS + b * EDGE
                lines.append(edges[at : at + EDGE])
            parts.append(jnp.concatenate(lines, axis=0).astype(bf16))
            rows = dot(relays[...], jnp.concatenate(parts, axis=0))
            for side in range(2):
                to = side * RELAY_ROWS + b * RELAY
                small_relay[to : to + RELAY] = rows[side * RELAY : (side + 1) * RELAY]
        sbuf[step, RELAY_AT:SENT] = small_relay[...].astype(bf16)
        for copy in relayed[step]:
            copy.start()

    small[...] = jnp.zeros(small.shape, f32)
    small_ham[...] = jnp.zeros(small_ham.shape, f32)
    small_relay[...] = jnp.zeros(small_relay.shape, f32)
    for step in range(5):
        rbuf[step, SENT:GHOST] = jnp.zeros((GHOST - SENT, LANES), bf16)
    pack(0, lambda b: dot(picks[0:DIRECT], noise[b]))
    pl.semaphore_wait(barrier, COPIES)
    for copy in flying[0]:
        copy.start()

    for b in range(ORB):
        turned = noise[b].astype(f32).T
        chain[0, :, b * LANES : (b + 1) * LANES] = turned
        ext_own[0:LANES, b * LANES : (b + 1) * LANES] = turned.astype(bf16)
        noise_ext[b * LANES : (b + 1) * LANES, 0:LANES] = turned.astype(bf16)

    @pl.loop(0, EXT // LANES)
    def _(part):
        first = pl.multiple_of(part * LANES, LANES)
        rows = lax.broadcasted_iota(jnp.int32, (LANES, LANES), 0) + first
        for m in range(NEIGH):
            same = rows == index[m : m + 1, :]
            onehot[pl.ds(first, LANES), m * LANES : (m + 1) * LANES] = jnp.where(
                same, 1.0, 0.0
            ).astype(bf16)

    @pl.loop(0, (LANES + PICKED) // 8)
    def _(part):
        first = pl.multiple_of(part * 8, 8)
        rows = lax.broadcasted_iota(jnp.int32, (8, LANES), 0) + first
        for found, low in ((near_slot, 1), (far_slot, 8)):
            which = jnp.full((8, LANES), 7, jnp.int32)
            for at in range(7):
                which = jnp.where(rows == index[low + at : low + at + 1, :], at, which)
            found[pl.ds(first, 8)] = which

    def fill_columns(a):
        columns = pl.ds(pl.multiple_of(a * LANES, LANES), LANES)
        last = lax.broadcasted_iota(jnp.int32, (8, LANES), 0) == 7

        def fill_block(b):
            blocks = ham[a, b].astype(f32)
            itself = blocks[0:1]
            tables = []
            for low in (1, 8):
                rows = jnp.concatenate([blocks[low : low + 7], blocks[0:1]], axis=0)
                tables.append(jnp.where(last, 0.0, rows))

            def block(first, count):
                made = []
                for at in range(first, first + count, 8):
                    made.append(
                        jnp.take_along_axis(tables[0], near_slot[at : at + 8], axis=0)
                        + jnp.take_along_axis(tables[1], far_slot[at : at + 8], axis=0)
                    )
                return jnp.concatenate(made, axis=0)

            own = block(0, LANES)
            shape = (LANES, LANES)
            same = lax.broadcasted_iota(jnp.int32, shape, 0) == lax.broadcasted_iota(
                jnp.int32, shape, 1
            )
            own = jnp.where(same, itself, own)
            ht_own[pl.ds(pl.multiple_of(b * LANES, LANES), LANES), columns] = own.astype(bf16)
            for f in range(FACES):
                to = pl.multiple_of((f * ORB + b) * FACE, FACE)
                made = block(LANES + f * FACE, FACE)
                ht_ghost[pl.ds(to, FACE), columns] = made.astype(bf16)
            for e in range(EDGES):
                to = pl.multiple_of(e * EDGE_ROWS + b * EDGE, EDGE)
                small_ham[pl.ds(to, EDGE)] = block(LANES + FACES * FACE + e * EDGE, EDGE)
            for side in range(2):
                to = pl.multiple_of(RELAY_AT - EDGE_AT + side * RELAY_ROWS + b * RELAY, 8)
                small_ham[pl.ds(to, RELAY)] = block(LANES + DIRECT + side * RELAY, RELAY)

        @pl.loop(0, ORB // 3)
        def _(group):
            for at in range(3):
                fill_block(group * 3 + at)

        ht_ghost[EDGE_AT:GHOST, columns] = small_ham[...].astype(bf16)

    pl.loop(0, 5)(fill_columns)
    pass_on(0)
    pl.loop(5, ORB)(fill_columns)

    def multiply(rows, ext, operator, first, span=slice(None)):
        def share(columns):
            product = dot(ext[rows, span], operator[span, columns])
            if first:
                acc[rows, columns] = product
            else:
                acc[rows, columns] += product

        @pl.loop(0, 2)
        def _(part):
            share(pl.ds(pl.multiple_of(part * 4 * LANES, 4 * LANES), 4 * LANES))

        share(slice(8 * LANES, WIDE))

    def multiply_ghosts(step, rows):
        if step > 0:
            pass_on(step)
        ext_ghost[rows, 0:RELAY_AT] = rbuf[step, 0:RELAY_AT].T
        multiply(rows, ext_ghost, ht_ghost, False, slice(0, RELAY_AT))
        for copy in relayed[step]:
            copy.wait_recv()
        ext_ghost[rows, RELAY_AT:GHOST] = rbuf[step, RELAY_AT:GHOST].T
        multiply(rows, ext_ghost, ht_ghost, False, slice(RELAY_AT, GHOST))

    vectors = (slice(0, HALF), slice(HALF, LANES))
    pieces = (slice(0, LANES), slice(LANES, 2 * LANES))

    def summed(half):
        base = half * LANES
        return acc[base : base + HALF] + acc[base + HALF : base + LANES]

    def send_half(order, half):
        high, low = halves(chain[order, vectors[half]])
        ext_own[half * LANES : half * LANES + HALF] = high
        ext_own[half * LANES + HALF : (half + 1) * LANES] = low
        step = 2 * order - 1 + half
        pack(
            step,
            lambda b: dot_t(picks[0:DIRECT], ext_own[pieces[half], b * LANES : (b + 1) * LANES]),
        )
        for copy in flying[step]:
            copy.start()

    multiply(pieces[0], ext_own, ht_own, True)
    multiply_ghosts(0, pieces[0])
    chain[1] = acc[0:LANES]
    send_half(1, 0)
    send_half(1, 1)
    res[...] = coef[0] * chain[0] + coef[1] * chain[1]

    for b in range(ORB):
        parts = []
        for f in range(FACES):
            at = (f * ORB + b) * FACE
            parts.append(rbuf[0, at : at + FACE])
        noise_rows = jnp.concatenate(parts, axis=0)
        noise_ext[b * LANES : (b + 1) * LANES, LANES : LANES + FACES * FACE] = noise_rows.T
    small_ghost = rbuf[0, EDGE_AT:GHOST].astype(f32)
    for b in range(ORB):
        parts = []
        for e in range(EDGES):
            at = e * EDGE_ROWS + b * EDGE
            parts.append(small_ghost[at : at + EDGE])
        for side in range(2):
            at = RELAY_AT - EDGE_AT + side * RELAY_ROWS + b * RELAY
            parts.append(small_ghost[at : at + RELAY])
        parts.append(jnp.zeros((EXT - LANES - PICKED, LANES), f32))
        noise_rows = jnp.concatenate(parts, axis=0).astype(bf16)
        noise_ext[b * LANES : (b + 1) * LANES, LANES + FACES * FACE : EXT] = noise_rows.T

    multiply(slice(0, 2 * LANES), ext_own, ht_own, True)

    @pl.loop(0, (NEIGH - 1) // 2)
    def _(two):
        hot = onehot[:, pl.ds(pl.multiple_of(two * 2 * LANES + LANES, LANES), 2 * LANES)]
        both = dot(noise_ext[...], hot).astype(bf16)
        gathered[2 * two] = both[:, 0:LANES]
        gathered[2 * two + 1] = both[:, LANES:]

    for half in range(2):
        multiply_ghosts(1 + half, pieces[half])
        chain[2, vectors[half]] = 2.0 * summed(half) - chain[0, vectors[half]]
        send_half(2, half)
        multiply(pieces[half], ext_own, ht_own, True)
    res[...] += coef[2] * chain[2]

    dens[:, 0:1] = jnp.zeros((ORB * ORB, 1, LANES), f32)

    for half in range(2):
        multiply_ghosts(3 + half, pieces[half])
        res[vectors[half]] += coef[3] * (2.0 * summed(half) - chain[1, vectors[half]])

        @pl.loop(1, NEIGH)
        def _(m):
            @pl.loop(0, ORB // 3)
            def _(group):
                for at in range(3):
                    b = group * 3 + at
                    base = pl.multiple_of(b * LANES + half * HALF, HALF)
                    near = gathered[m - 1, pl.ds(base, HALF)].astype(f32)
                    for a in range(ORB):
                        term = res[vectors[half], a * LANES : (a + 1) * LANES] * near
                        row = jnp.sum(term, axis=0, keepdims=True)
                        if half == 0:
                            dens[a * ORB + b, pl.ds(m, 1)] = row
                        else:
                            dens[a * ORB + b, pl.ds(m, 1)] += row

    pairs[...] = jnp.zeros(pairs.shape, f32)
    for c in range(3):
        def add(ab, total):
            return total + deriv[c, ab].astype(f32) * dens[ab, 0:NEIGH]

        total = lax.fori_loop(0, ORB * ORB, add, jnp.zeros((NEIGH, LANES), f32), unroll=9)
        pair = total * (1.0 / LANES)
        pairs[c : c + 1, 0:LANES] = -jnp.sum(pair, axis=0, keepdims=True)
        for m in range(1, NEIGH):
            pairs[c : c + 1, m * LANES : (m + 1) * LANES] = pair[m : m + 1]
    high, low = halves(pairs[...])
    spread = dot_t(onehot[...], jnp.concatenate([high, low], axis=0)).T
    spread = spread[0:8] + spread[8:16]
    high, low = halves(spread[:, LANES:EXT])
    mask = spans[...]
    shape = (COPIES * 8, SHARE)
    high = (high.astype(f32)[None] * mask).reshape(shape).astype(bf16)
    low = (low.astype(f32)[None] * mask).reshape(shape).astype(bf16)
    tiles = dot(high[:, 0:PICKED], picks[...]) + dot(low[:, 0:PICKED], picks[...])
    fsend[...] = tiles.reshape(COPIES, 8, LANES)

    back = []
    for at, (direction, _, _) in enumerate(SEGMENTS):
        back.append(
            pltpu.make_async_remote_copy(
                src_ref=fsend.at[at],
                dst_ref=frecv.at[at],
                send_sem=send_sem.at[5, at],
                recv_sem=recv_sem.at[5, at],
                device_id=shifted(direction, 1),
                device_id_type=MESH,
            )
        )
    for copy in back:
        copy.start()
    for a in range(ORB):
        w_out[a] = res[:, a * LANES : (a + 1) * LANES].T
    for copy in back:
        copy.wait_recv()
    total = spread[:, 0:LANES]
    for at in range(COPIES):
        total = total + frecv[at]
    f_out[...] = total[0:3]
    for group in flying + relayed:
        for copy in group:
            copy.wait_send()
    for copy in back:
        copy.wait_send()


def extended_slots(sizes, neighbours):
    atom_count = neighbours.shape[0]
    cell_count = CX * CY * CZ
    size_x, size_y, size_z = sizes
    ids = neighbours.T
    domain = ids // atom_count
    within = ids % atom_count
    basis = within // cell_count
    remain = within % cell_count
    parts = (
        (domain // (size_y * size_z), remain // (CY * CZ), "gx", CX, size_x),
        (domain // size_z % size_y, remain // CZ % CY, "gy", CY, size_y),
        (domain % size_z, remain % CZ, "gz", CZ, size_z),
    )
    signs = []
    inside = basis
    for dom, cell, axis, cells, size in parts:
        place = jnp.remainder((dom - lax.axis_index(axis)) * cells + cell + 1, cells * size)
        sign = jnp.where(place == 0, -1, jnp.where(place == cells + 1, 1, 0))
        signs.append(sign)
        inside = jnp.where(sign == 0, inside * cells + place - 1, inside)
    code = signs[0] * 9 + signs[1] * 3 + signs[2]
    first = jnp.zeros_like(code)
    for (dx, dy, dz), row, _ in SEGMENTS:
        first = jnp.where(code == dx * 9 + dy * 3 + dz, LANES + row, first)
    return first + inside


def shards(sizes, noise, ham, deriv, neighbours, coef):
    f32 = jnp.float32
    bf16 = jnp.bfloat16
    index = extended_slots(sizes, neighbours)
    ham = ham.transpose(1, 2, 0, 3)
    deriv = deriv.transpose(0, 2, 3, 1, 4).reshape(3, ORB * ORB, NEIGH, LANES)
    picks = jnp.asarray(picking_matrix(), bf16)
    relays = jnp.asarray(relaying_matrix(), bf16)
    spans = jnp.asarray(segment_spans(), f32)
    vmem = pl.BlockSpec(memory_space=pltpu.VMEM)
    smem = pl.BlockSpec(memory_space=pltpu.SMEM)
    return pl.pallas_call(
        functools.partial(kernel, sizes),
        out_shape=(
            jax.ShapeDtypeStruct((ORB, LANES, LANES), f32),
            jax.ShapeDtypeStruct((3, LANES), f32),
        ),
        in_specs=[vmem, vmem, vmem, vmem, smem, vmem, vmem, vmem],
        out_specs=(vmem, vmem),
        scratch_shapes=[
            pltpu.VMEM((WIDE, WIDE), bf16),
            pltpu.VMEM((GHOST, WIDE), bf16),
            pltpu.VMEM((EXT, NEIGH * LANES), bf16),
            pltpu.VMEM((2 * LANES, WIDE), bf16),
            pltpu.VMEM((2 * LANES, GHOST), bf16),
            pltpu.VMEM((WIDE, EXT), bf16),
            pltpu.VMEM((NEIGH - 1, WIDE, LANES), bf16),
            pltpu.VMEM((3, LANES, WIDE), f32),
            pltpu.VMEM((LANES, WIDE), f32),
            pltpu.VMEM((2 * LANES, WIDE), f32),
            pltpu.VMEM((5, SENT, LANES), bf16),
            pltpu.VMEM((5, GHOST, LANES), bf16),
            pltpu.VMEM((EDGES * EDGE_ROWS, LANES), f32),
            pltpu.VMEM((SMALL, LANES), f32),
            pltpu.VMEM((2 * RELAY_ROWS, LANES), f32),
            pltpu.VMEM((LANES + PICKED, LANES), jnp.int32),
            pltpu.VMEM((LANES + PICKED, LANES), jnp.int32),
            pltpu.VMEM((COPIES, 8, LANES), f32),
            pltpu.VMEM((COPIES, 8, LANES), f32),
            pltpu.VMEM((8, NEIGH * LANES), f32),
            pltpu.VMEM((ORB * ORB, 16, LANES), f32),
            pltpu.SemaphoreType.DMA((6, COPIES)),
            pltpu.SemaphoreType.DMA((6, COPIES)),
        ],
        compiler_params=pltpu.CompilerParams(
            collective_id=0, has_side_effects=True, vmem_limit_bytes=56 * 1024 * 1024
        ),
        name="fermi_forces",
    )(noise, ham, deriv, index, coef, picks, relays, spans)


def solution(mesh):
    sizes = tuple(mesh.shape[name] for name in ("gx", "gy", "gz"))
    in_specs = (
        P(None, ("gx", "gy", "gz"), None),
        P(None, None, None, ("gx", "gy", "gz")),
        P(None, None, None, None, ("gx", "gy", "gz")),
        P(("gx", "gy", "gz"), None),
        P(),
    )
    out_specs = (P(None, ("gx", "gy", "gz"), None), P(None, ("gx", "gy", "gz")))
    return jax.shard_map(
        functools.partial(shards, sizes),
        mesh=mesh,
        in_specs=in_specs,
        out_specs=out_specs,
        check_vma=False,
    )
```

```python
import functools

import jax
import jax.numpy as jnp
import numpy as np
from jax import lax
from jax.experimental import pallas as pl
from jax.experimental.pallas import tpu as pltpu
from jax.sharding import PartitionSpec as P

MESH = pl.DeviceIdType.MESH
CX = 4
CY = 4
CZ = 4
NEIGH = 15
ORB = 9
LANES = 128
HALF = 64
WIDE = ORB * LANES
FACE = 32
EDGE = 8
CORNER = 2
FACES = 6
EDGES = 4
DIRECT = FACES * FACE + EDGES * EDGE
RELAY = 4 * EDGE + 4 * CORNER
PICKED = DIRECT + 2 * RELAY
EXT = 512
FACE_ROWS = ORB * FACE
EDGE_ROWS = 80
RELAY_ROWS = 368
EDGE_AT = FACES * FACE_ROWS
RELAY_AT = EDGE_AT + EDGES * EDGE_ROWS
SENT = RELAY_AT + 2 * RELAY_ROWS
GHOST = SENT + 32
SMALL = GHOST - EDGE_AT
SHARE = 384
HELD = ((-1, 0, 0), (1, 0, 0), (0, 0, -1), (0, 0, 1), (-1, 0, -1), (-1, 0, 1), (1, 0, -1), (1, 0, 1))


def ghost_segments():
    order = HELD[0:4] + ((0, -1, 0), (0, 1, 0)) + HELD[4:8]
    for dy in (-1, 1):
        order = order + tuple((dx, dy, dz) for dx, _, dz in HELD)
    placed = []
    first = 0
    for direction in order:
        placed.append((direction, first, atoms_in(direction)))
        first += atoms_in(direction)
    return placed


def atoms_in(direction):
    return (FACE, EDGE, CORNER)[sum(abs(d) for d in direction) - 1]


SEGMENTS = ghost_segments()
COPIES = len(SEGMENTS)


def cells_of(d, cells):
    return range(cells) if d == 0 else ((0,) if d > 0 else (cells - 1,))


def picking_matrix():
    picks = np.zeros((PICKED, LANES), np.float32)
    row = 0
    for (dx, dy, dz), _, _ in SEGMENTS:
        for basis in range(2):
            for x in cells_of(dx, CX):
                for y in cells_of(dy, CY):
                    for z in cells_of(dz, CZ):
                        picks[row, ((basis * CX + x) * CY + y) * CZ + z] = 1.0
                        row += 1
    return picks


def relaying_matrix():
    picks = np.zeros((2 * RELAY, 4 * FACE + 4 * EDGE), np.float32)
    row = 0
    for dy in (-1, 1):
        held = 0
        for dx, _, dz in HELD:
            for basis in range(2):
                for x in cells_of(dx, CX):
                    for y in range(CY):
                        for z in cells_of(dz, CZ):
                            if y in cells_of(dy, CY):
                                picks[row, held] = 1.0
                                row += 1
                            held += 1
    return picks


def segment_spans():
    spans = np.zeros((COPIES, 8, SHARE), np.float32)
    for at, (_, first, count) in enumerate(SEGMENTS):
        spans[at, :, first : first + count] = 1.0
    return spans


def dot(a, b):
    return jnp.dot(a, b, preferred_element_type=jnp.float32)


def dot_t(a, b):
    return lax.dot_general(a, b, (((1,), (1,)), ((), ())), preferred_element_type=jnp.float32)


def halves(x):
    high = x.astype(jnp.bfloat16)
    return high, (x - high.astype(jnp.float32)).astype(jnp.bfloat16)


def kernel(
    sizes,
    noise,
    ham,
    deriv,
    index,
    coef,
    picks,
    relays,
    spans,
    w_out,
    f_out,
    ht_own,
    ht_ghost,
    onehot,
    ext_own,
    ext_ghost,
    noise_ext,
    gathered,
    chain,
    res,
    acc,
    sbuf,
    rbuf,
    small,
    small_ham,
    small_relay,
    near_slot,
    far_slot,
    fsend,
    frecv,
    pairs,
    dens,
    send_sem,
    recv_sem,
):
    f32 = jnp.float32
    bf16 = jnp.bfloat16
    here = [lax.axis_index(name) for name in ("gx", "gy", "gz")]

    def shifted(direction, sign):
        return tuple(
            lax.rem(me + size + sign * d, size) for me, size, d in zip(here, sizes, direction)
        )

    barrier = pltpu.get_barrier_semaphore()
    for direction, _, _ in SEGMENTS:
        pl.semaphore_signal(barrier, inc=1, device_id=shifted(direction, -1), device_id_type=MESH)

    def pack(step, rows_of):
        for b in range(ORB):
            rows = rows_of(b)
            for f in range(FACES):
                to = (f * ORB + b) * FACE
                sbuf[step, to : to + FACE] = rows[f * FACE : (f + 1) * FACE].astype(bf16)
            for e in range(EDGES):
                at = FACES * FACE + e * EDGE
                to = e * EDGE_ROWS + b * EDGE
                small[to : to + EDGE] = rows[at : at + EDGE]
        sbuf[step, EDGE_AT:RELAY_AT] = small[0 : EDGES * EDGE_ROWS].astype(bf16)

    def copy_rows(step, at, first, rows, direction):
        return pltpu.make_async_remote_copy(
            src_ref=sbuf.at[step, pl.ds(first, rows), :],
            dst_ref=rbuf.at[step, pl.ds(first, rows), :],
            send_sem=send_sem.at[step, at],
            recv_sem=recv_sem.at[step, at],
            device_id=shifted(direction, -1),
            device_id_type=MESH,
        )

    def copies(step):
        made = []
        for at, (direction, _, _) in enumerate(SEGMENTS[0 : FACES + EDGES]):
            if at < FACES:
                made.append(copy_rows(step, at, at * FACE_ROWS, FACE_ROWS, direction))
            else:
                first = EDGE_AT + (at - FACES) * EDGE_ROWS
                made.append(copy_rows(step, at, first, EDGE_ROWS, direction))
        return made

    def relay_copies(step):
        made = []
        for at, dy in enumerate((-1, 1)):
            first = RELAY_AT + at * RELAY_ROWS
            made.append(copy_rows(step, FACES + EDGES + at, first, RELAY_ROWS, (0, dy, 0)))
        return made

    flying = [copies(step) for step in range(5)]
    relayed = [relay_copies(step) for step in range(5)]

    def pass_on(step):
        for copy in flying[step]:
            copy.wait_recv()
        edges = rbuf[step, EDGE_AT:RELAY_AT].astype(f32)
        for b in range(ORB):
            parts = []
            for f in range(4):
                at = (f * ORB + b) * FACE
                parts.append(rbuf[step, at : at + FACE])
            lines = []
            for e in range(EDGES):
                at = e * EDGE_ROWS + b * EDGE
                lines.append(edges[at : at + EDGE])
            parts.append(jnp.concatenate(lines, axis=0).astype(bf16))
            rows = dot(relays[...], jnp.concatenate(parts, axis=0))
            for side in range(2):
                to = side * RELAY_ROWS + b * RELAY
                small_relay[to : to + RELAY] = rows[side * RELAY : (side + 1) * RELAY]
        sbuf[step, RELAY_AT:SENT] = small_relay[...].astype(bf16)
        for copy in relayed[step]:
            copy.start()

    small[...] = jnp.zeros(small.shape, f32)
    small_ham[...] = jnp.zeros(small_ham.shape, f32)
    small_relay[...] = jnp.zeros(small_relay.shape, f32)
    for step in range(5):
        rbuf[step, SENT:GHOST] = jnp.zeros((GHOST - SENT, LANES), bf16)
    pack(0, lambda b: dot(picks[0:DIRECT], noise[b]))
    pl.semaphore_wait(barrier, COPIES)
    for copy in flying[0]:
        copy.start()

    for b in range(ORB):
        turned = noise[b].astype(f32).T
        chain[0, :, b * LANES : (b + 1) * LANES] = turned
        ext_own[0:LANES, b * LANES : (b + 1) * LANES] = turned.astype(bf16)
        noise_ext[b * LANES : (b + 1) * LANES, 0:LANES] = turned.astype(bf16)

    @pl.loop(0, EXT // LANES)
    def _(part):
        first = pl.multiple_of(part * LANES, LANES)
        rows = lax.broadcasted_iota(jnp.int32, (LANES, LANES), 0) + first
        for m in range(NEIGH):
            same = rows == index[m : m + 1, :]
            onehot[pl.ds(first, LANES), m * LANES : (m + 1) * LANES] = jnp.where(
                same, 1.0, 0.0
            ).astype(bf16)

    @pl.loop(0, (LANES + PICKED) // 8)
    def _(part):
        first = pl.multiple_of(part * 8, 8)
        rows = lax.broadcasted_iota(jnp.int32, (8, LANES), 0) + first
        for found, low in ((near_slot, 1), (far_slot, 8)):
            which = jnp.full((8, LANES), 7, jnp.int32)
            for at in range(7):
                which = jnp.where(rows == index[low + at : low + at + 1, :], at, which)
            found[pl.ds(first, 8)] = which

    def fill_columns(a):
        columns = pl.ds(pl.multiple_of(a * LANES, LANES), LANES)
        last = lax.broadcasted_iota(jnp.int32, (8, LANES), 0) == 7

        def fill_block(b):
            blocks = ham[a, b].astype(f32)
            itself = blocks[0:1]
            tables = []
            for low in (1, 8):
                rows = jnp.concatenate([blocks[low : low + 7], blocks[0:1]], axis=0)
                tables.append(jnp.where(last, 0.0, rows))

            def block(first, count):
                made = []
                for at in range(first, first + count, 8):
                    made.append(
                        jnp.take_along_axis(tables[0], near_slot[at : at + 8], axis=0)
                        + jnp.take_along_axis(tables[1], far_slot[at : at + 8], axis=0)
                    )
                return jnp.concatenate(made, axis=0)

            own = block(0, LANES)
            shape = (LANES, LANES)
            same = lax.broadcasted_iota(jnp.int32, shape, 0) == lax.broadcasted_iota(
                jnp.int32, shape, 1
            )
            own = jnp.where(same, itself, own)
            ht_own[pl.ds(pl.multiple_of(b * LANES, LANES), LANES), columns] = own.astype(bf16)
            for f in range(FACES):
                to = pl.multiple_of((f * ORB + b) * FACE, FACE)
                made = block(LANES + f * FACE, FACE)
                ht_ghost[pl.ds(to, FACE), columns] = made.astype(bf16)
            for e in range(EDGES):
                to = pl.multiple_of(e * EDGE_ROWS + b * EDGE, EDGE)
                small_ham[pl.ds(to, EDGE)] = block(LANES + FACES * FACE + e * EDGE, EDGE)
            for side in range(2):
                to = pl.multiple_of(RELAY_AT - EDGE_AT + side * RELAY_ROWS + b * RELAY, 8)
                small_ham[pl.ds(to, RELAY)] = block(LANES + DIRECT + side * RELAY, RELAY)

        @pl.loop(0, ORB // 3)
        def _(group):
            for at in range(3):
                fill_block(group * 3 + at)

        ht_ghost[EDGE_AT:GHOST, columns] = small_ham[...].astype(bf16)

    pl.loop(0, 5)(fill_columns)
    pass_on(0)
    pl.loop(5, ORB)(fill_columns)

    def multiply(rows, ext, operator, first, span=slice(None)):
        def share(columns):
            product = dot(ext[rows, span], operator[span, columns])
            if first:
                acc[rows, columns] = product
            else:
                acc[rows, columns] += product

        @pl.loop(0, 2)
        def _(part):
            share(pl.ds(pl.multiple_of(part * 4 * LANES, 4 * LANES), 4 * LANES))

        share(slice(8 * LANES, WIDE))

    def multiply_ghosts(step, rows):
        ext_ghost[rows, 0:RELAY_AT] = rbuf[step, 0:RELAY_AT].T
        multiply(rows, ext_ghost, ht_ghost, False, slice(0, RELAY_AT))
        for copy in relayed[step]:
            copy.wait_recv()
        ext_ghost[rows, RELAY_AT:GHOST] = rbuf[step, RELAY_AT:GHOST].T
        multiply(rows, ext_ghost, ht_ghost, False, slice(RELAY_AT, GHOST))

    vectors = (slice(0, HALF), slice(HALF, LANES))
    pieces = (slice(0, LANES), slice(LANES, 2 * LANES))

    def summed(half):
        base = half * LANES
        return acc[base : base + HALF] + acc[base + HALF : base + LANES]

    def send_half(order, half):
        high, low = halves(chain[order, vectors[half]])
        ext_own[half * LANES : half * LANES + HALF] = high
        ext_own[half * LANES + HALF : (half + 1) * LANES] = low
        step = 2 * order - 1 + half
        pack(
            step,
            lambda b: dot_t(picks[0:DIRECT], ext_own[pieces[half], b * LANES : (b + 1) * LANES]),
        )
        for copy in flying[step]:
            copy.start()

    multiply(pieces[0], ext_own, ht_own, True)
    multiply_ghosts(0, pieces[0])
    chain[1] = acc[0:LANES]
    send_half(1, 0)
    send_half(1, 1)
    res[...] = coef[0] * chain[0] + coef[1] * chain[1]

    for b in range(ORB):
        parts = []
        for f in range(FACES):
            at = (f * ORB + b) * FACE
            parts.append(rbuf[0, at : at + FACE])
        noise_rows = jnp.concatenate(parts, axis=0)
        noise_ext[b * LANES : (b + 1) * LANES, LANES : LANES + FACES * FACE] = noise_rows.T
    small_ghost = rbuf[0, EDGE_AT:GHOST].astype(f32)
    for b in range(ORB):
        parts = []
        for e in range(EDGES):
            at = e * EDGE_ROWS + b * EDGE
            parts.append(small_ghost[at : at + EDGE])
        for side in range(2):
            at = RELAY_AT - EDGE_AT + side * RELAY_ROWS + b * RELAY
            parts.append(small_ghost[at : at + RELAY])
        parts.append(jnp.zeros((EXT - LANES - PICKED, LANES), f32))
        noise_rows = jnp.concatenate(parts, axis=0).astype(bf16)
        noise_ext[b * LANES : (b + 1) * LANES, LANES + FACES * FACE : EXT] = noise_rows.T

    multiply(slice(0, 2 * LANES), ext_own, ht_own, True)

    def gather(two):
        hot = onehot[:, pl.ds(pl.multiple_of(two * 2 * LANES + LANES, LANES), 2 * LANES)]
        both = dot(noise_ext[...], hot).astype(bf16)
        gathered[2 * two] = both[:, 0:LANES]
        gathered[2 * two + 1] = both[:, LANES:]

    pl.loop(0, 3)(gather)
    pass_on(1)
    pl.loop(3, (NEIGH - 1) // 2)(gather)

    for half in range(2):
        multiply_ghosts(1 + half, pieces[half])
        chain[2, vectors[half]] = 2.0 * summed(half) - chain[0, vectors[half]]
        send_half(2, half)
        pass_on(2 + half)
        multiply(pieces[half], ext_own, ht_own, True)
    res[...] += coef[2] * chain[2]

    dens[:, 0:1] = jnp.zeros((ORB * ORB, 1, LANES), f32)

    for half in range(2):
        multiply_ghosts(3 + half, pieces[half])
        res[vectors[half]] += coef[3] * (2.0 * summed(half) - chain[1, vectors[half]])

        def densities(m):
            @pl.loop(0, ORB // 3)
            def _(group):
                for at in range(3):
                    b = group * 3 + at
                    base = pl.multiple_of(b * LANES + half * HALF, HALF)
                    near = gathered[m - 1, pl.ds(base, HALF)].astype(f32)
                    for a in range(ORB):
                        term = res[vectors[half], a * LANES : (a + 1) * LANES] * near
                        row = jnp.sum(term, axis=0, keepdims=True)
                        if half == 0:
                            dens[a * ORB + b, pl.ds(m, 1)] = row
                        else:
                            dens[a * ORB + b, pl.ds(m, 1)] += row

        if half == 0:
            pl.loop(1, 8)(densities)
            pass_on(4)
            pl.loop(8, NEIGH)(densities)
        else:
            pl.loop(1, NEIGH)(densities)

    pairs[...] = jnp.zeros(pairs.shape, f32)
    for c in range(3):
        def add(ab, total):
            return total + deriv[c, ab].astype(f32) * dens[ab, 0:NEIGH]

        total = lax.fori_loop(0, ORB * ORB, add, jnp.zeros((NEIGH, LANES), f32), unroll=9)
        pair = total * (1.0 / LANES)
        pairs[c : c + 1, 0:LANES] = -jnp.sum(pair, axis=0, keepdims=True)
        for m in range(1, NEIGH):
            pairs[c : c + 1, m * LANES : (m + 1) * LANES] = pair[m : m + 1]
    high, low = halves(pairs[...])
    spread = dot_t(onehot[...], jnp.concatenate([high, low], axis=0)).T
    spread = spread[0:8] + spread[8:16]
    high, low = halves(spread[:, LANES:EXT])
    mask = spans[...]
    shape = (COPIES * 8, SHARE)
    high = (high.astype(f32)[None] * mask).reshape(shape).astype(bf16)
    low = (low.astype(f32)[None] * mask).reshape(shape).astype(bf16)
    tiles = dot(high[:, 0:PICKED], picks[...]) + dot(low[:, 0:PICKED], picks[...])
    fsend[...] = tiles.reshape(COPIES, 8, LANES)

    back = []
    for at, (direction, _, _) in enumerate(SEGMENTS):
        back.append(
            pltpu.make_async_remote_copy(
                src_ref=fsend.at[at],
                dst_ref=frecv.at[at],
                send_sem=send_sem.at[5, at],
                recv_sem=recv_sem.at[5, at],
                device_id=shifted(direction, 1),
                device_id_type=MESH,
            )
        )
    for copy in back:
        copy.start()
    for a in range(ORB):
        w_out[a] = res[:, a * LANES : (a + 1) * LANES].T
    for copy in back:
        copy.wait_recv()
    total = spread[:, 0:LANES]
    for at in range(COPIES):
        total = total + frecv[at]
    f_out[...] = total[0:3]
    for group in flying + relayed:
        for copy in group:
            copy.wait_send()
    for copy in back:
        copy.wait_send()


def extended_slots(sizes, neighbours):
    atom_count = neighbours.shape[0]
    cell_count = CX * CY * CZ
    size_x, size_y, size_z = sizes
    ids = neighbours.T
    domain = ids // atom_count
    within = ids % atom_count
    basis = within // cell_count
    remain = within % cell_count
    parts = (
        (domain // (size_y * size_z), remain // (CY * CZ), "gx", CX, size_x),
        (domain // size_z % size_y, remain // CZ % CY, "gy", CY, size_y),
        (domain % size_z, remain % CZ, "gz", CZ, size_z),
    )
    signs = []
    inside = basis
    for dom, cell, axis, cells, size in parts:
        place = jnp.remainder((dom - lax.axis_index(axis)) * cells + cell + 1, cells * size)
        sign = jnp.where(place == 0, -1, jnp.where(place == cells + 1, 1, 0))
        signs.append(sign)
        inside = jnp.where(sign == 0, inside * cells + place - 1, inside)
    code = signs[0] * 9 + signs[1] * 3 + signs[2]
    first = jnp.zeros_like(code)
    for (dx, dy, dz), row, _ in SEGMENTS:
        first = jnp.where(code == dx * 9 + dy * 3 + dz, LANES + row, first)
    return first + inside


def shards(sizes, noise, ham, deriv, neighbours, coef):
    f32 = jnp.float32
    bf16 = jnp.bfloat16
    index = extended_slots(sizes, neighbours)
    ham = ham.transpose(1, 2, 0, 3)
    deriv = deriv.transpose(0, 2, 3, 1, 4).reshape(3, ORB * ORB, NEIGH, LANES)
    picks = jnp.asarray(picking_matrix(), bf16)
    relays = jnp.asarray(relaying_matrix(), bf16)
    spans = jnp.asarray(segment_spans(), f32)
    vmem = pl.BlockSpec(memory_space=pltpu.VMEM)
    smem = pl.BlockSpec(memory_space=pltpu.SMEM)
    return pl.pallas_call(
        functools.partial(kernel, sizes),
        out_shape=(
            jax.ShapeDtypeStruct((ORB, LANES, LANES), f32),
            jax.ShapeDtypeStruct((3, LANES), f32),
        ),
        in_specs=[vmem, vmem, vmem, vmem, smem, vmem, vmem, vmem],
        out_specs=(vmem, vmem),
        scratch_shapes=[
            pltpu.VMEM((WIDE, WIDE), bf16),
            pltpu.VMEM((GHOST, WIDE), bf16),
            pltpu.VMEM((EXT, NEIGH * LANES), bf16),
            pltpu.VMEM((2 * LANES, WIDE), bf16),
            pltpu.VMEM((2 * LANES, GHOST), bf16),
            pltpu.VMEM((WIDE, EXT), bf16),
            pltpu.VMEM((NEIGH - 1, WIDE, LANES), bf16),
            pltpu.VMEM((3, LANES, WIDE), f32),
            pltpu.VMEM((LANES, WIDE), f32),
            pltpu.VMEM((2 * LANES, WIDE), f32),
            pltpu.VMEM((5, SENT, LANES), bf16),
            pltpu.VMEM((5, GHOST, LANES), bf16),
            pltpu.VMEM((EDGES * EDGE_ROWS, LANES), f32),
            pltpu.VMEM((SMALL, LANES), f32),
            pltpu.VMEM((2 * RELAY_ROWS, LANES), f32),
            pltpu.VMEM((LANES + PICKED, LANES), jnp.int32),
            pltpu.VMEM((LANES + PICKED, LANES), jnp.int32),
            pltpu.VMEM((COPIES, 8, LANES), f32),
            pltpu.VMEM((COPIES, 8, LANES), f32),
            pltpu.VMEM((8, NEIGH * LANES), f32),
            pltpu.VMEM((ORB * ORB, 16, LANES), f32),
            pltpu.SemaphoreType.DMA((6, COPIES)),
            pltpu.SemaphoreType.DMA((6, COPIES)),
        ],
        compiler_params=pltpu.CompilerParams(
            collective_id=0, has_side_effects=True, vmem_limit_bytes=56 * 1024 * 1024
        ),
        name="fermi_forces",
    )(noise, ham, deriv, index, coef, picks, relays, spans)


def solution(mesh):
    sizes = tuple(mesh.shape[name] for name in ("gx", "gy", "gz"))
    in_specs = (
        P(None, ("gx", "gy", "gz"), None),
        P(None, None, None, ("gx", "gy", "gz")),
        P(None, None, None, None, ("gx", "gy", "gz")),
        P(("gx", "gy", "gz"), None),
        P(),
    )
    out_specs = (P(None, ("gx", "gy", "gz"), None), P(None, ("gx", "gy", "gz")))
    return jax.shard_map(
        functools.partial(shards, sizes),
        mesh=mesh,
        in_specs=in_specs,
        out_specs=out_specs,
        check_vma=False,
    )
```
